256 devices in a mesh: date: 8 (over y, core), parcel: 32 (over x, z).
Axes of the slice: x: 4, y: 4, z: 8, core: 2. Of those that a mesh axis runs over, the one named last changes fastest.
Arguments:
- tile_pixels: bfloat16 [32, 4096, 640], P('date', 'parcel'), may hold values from -12 to 12
- owner: int32 [2048, 1], replicated, may hold values from 0 to 31; in each aligned block of 64 rows (0 to 63, 64 to 127, ...) at most 4 rows name the same one
- pix_count: int32 [2048], replicated, may hold values from 1 to 64
- cloud: int32 [2048, 32], P(('parcel', 'date')), may hold values 0 or 1
- w_pix1: bfloat16 [10, 128], replicated, may hold values from -2 to 2
- w_pix2: bfloat16 [128, 128], replicated, may hold values from -0.5 to 0.5
- w_embed: bfloat16 [256, 1024], replicated, may hold values from -2 to 2
- norm_gain: bfloat16 [1024], replicated, may hold values from 0.5 to 1.5
- w_qkv: bfloat16 [1024, 3072], replicated, may hold values from -0.1875 to 0.1875
- w_out: bfloat16 [1024, 1024], replicated, may hold values from -0.1875 to 0.1875
- head_scale: float32 [16], replicated, may hold values from 2 to 30
- logit_scale: float32 [1], replicated, may hold values from 5 to 30
- pos_ids: int32 [2048], P(('parcel', 'date')), may hold values from 0 to 255
- neg_ids: int32 [2048, 128], P(('parcel', 'date')), may hold values from 0 to 255
Outputs:
- parcel_embedding: bfloat16 [2048, 1024], P(('parcel', 'date'))
- contrast_loss: float32 [2048], P(('parcel', 'date'))
The draws below stay inside these ranges and needn't reach their ends.
Inputs may be any that keep to these rules, and one draw needn't show every extreme that they name: Among the 64 parcels of one parcel owner (aligned blocks), at most 4 share one tile owner; some owner reaches 4.
All inputs are finite; a program needn't handle non-finite values. No bound on the sum of `cloud` on one device may be relied on, other than what follows from the above.
Results may differ from the reference program's by a relative error of at most 0.007.
Values may be sent and summed in bfloat16 or wider, within the bound.
No kernel may reach another device: no remote copies, remote signals or barrier semaphores. Data moves between devices by JAX's collectives and lax.ppermute only.
A program may use at most 64 MiB of HBM per device.

```python
import math
import jax
import jax.numpy as jnp
import numpy as np
from jax import lax

D = 1024
H = 16
S = 64
C = 10
HP = 128
PAR_DEV = 64
NNEG = 128
PARCELS = 2048
DATES = 32
CAP = 4
GROUP = 256
N_DATE = 8
N_PARCEL = 32


def draw_tile_pixels(key, part):
    key = jax.random.fold_in(key, 11)
    noise_key, scale_key, offset_key, band_key = jax.random.split(key, 4)
    slot_total = N_PARCEL * N_PARCEL * CAP
    noise = jnp.clip(jax.random.normal(noise_key, (DATES, slot_total, S, C), jnp.float32), -3.0, 3.0)
    scale = jnp.exp(jax.random.uniform(scale_key, (slot_total, 1, 1), jnp.float32, -2.0, 1.0))
    offset = jnp.clip(1.5 * jax.random.normal(offset_key, (slot_total, 1, C), jnp.float32), -4.5, 4.5)
    band = jnp.exp(jax.random.uniform(band_key, (slot_total, 1, C), jnp.float32, -0.5, 0.5))
    values = offset[None] + (scale * band)[None] * noise
    values = jnp.clip(values, -12.0, 12.0)
    return values.reshape(DATES, slot_total, S * C).astype(jnp.bfloat16)


def draw_w_embed(key, part):
    key = jax.random.fold_in(key, 23)
    entry_key, column_key = jax.random.split(key, 2)
    fan_in = 2 * HP
    entries = jnp.clip(jax.random.normal(entry_key, (fan_in, D), jnp.float32), -4.0, 4.0)
    column_scale = jnp.exp(jax.random.uniform(column_key, (1, D), jnp.float32, -3.0, 0.4))
    values = entries * column_scale / jnp.sqrt(jnp.float32(fan_in))
    return jnp.clip(values, -2.0, 2.0).astype(jnp.bfloat16)


def touch_ends(result, rng, least, largest):
    longest = result.shape.index(max(result.shape))
    spots = []
    for shift in (0, 1):
        where = [jax.random.randint(jax.random.fold_in(rng, axis), (), 0, length) for axis, length in enumerate(result.shape)]
        where[longest] = (where[longest] + shift) % result.shape[longest]
        spots.append(tuple(where))
    return result.at[spots[0]].set(least).at[spots[1]].set(largest)


def routed_block(stream_key, own, number, rows, number_of, top, limit, skew):
    order = jax.random.permutation(stream_key, number_of)
    crowded, ordinary = load_shares(number_of, rows * top, limit, skew, True), load_shares(number_of, rows * top, limit, skew, False)
    places = jnp.arange(number_of)

    def named(tallies, offset_by):
        used = int((tallies > 0).sum())
        fixed = max(1, used // 4)
        moved = fixed + (places - fixed + offset_by * (used - fixed)) % max(1, number_of - fixed)
        return jnp.zeros((number_of,), jnp.int32).at[order[jnp.where(places < fixed, places, moved)]].set(jnp.asarray(tallies, jnp.int32))

    tallies = jnp.where(number % 4 == 0, named(crowded, number // 4), named(ordinary, number - number // 4 - 1))
    mixed = jax.random.permutation(jax.random.fold_in(own, 3), number_of)
    source_of, sink = mixed[0:number_of // 2 * 2:2], mixed[1:number_of // 2 * 2:2]
    slack = jnp.minimum(tallies[source_of] - 1, limit - tallies[sink]) // 2
    slack = jnp.where((source_of == order[0]) | (sink == order[0]) | (tallies[sink] == 0), 0, jnp.maximum(slack, 0))
    moved = jax.random.randint(jax.random.fold_in(own, 4), (number_of // 2,), 0, 1 << 20) % (slack + 1)
    tallies = tallies.at[source_of].add(-moved).at[sink].add(moved)
    items = jnp.searchsorted(jnp.cumsum(tallies), jnp.arange(rows * top), side="right").astype(jnp.int32)
    listing = items.reshape(top, rows).T
    listing = listing[jax.random.permutation(jax.random.fold_in(own, 1), rows)]
    offset_by = jax.random.randint(jax.random.fold_in(own, 2), (rows, 1), 0, top)
    return jnp.take_along_axis(listing, (jnp.arange(top)[None, :] + offset_by) % top, axis=1)


def load_shares(number_of, total, bound, lean, full):
    portions = [(1 << 20) // math.isqrt(rank ** lean) + 1 for rank in range(1, number_of + 1)]
    largest = bound if full else min(bound, max(-(-total // number_of), total * portions[0] // sum(portions)))
    least = 1 if total - largest >= number_of - 1 else 0
    holding, rest = [largest] + [least] * (number_of - 1), total - largest - least * (number_of - 1)
    while rest > 0:
        free = [i for i in range(1, number_of) if holding[i] < largest] or [i for i in range(1, number_of) if holding[i] < bound]
        whole, budget = sum([portions[i] for i in free]), rest
        for i in free:
            addition = min(bound - holding[i], max(1, budget * portions[i] // whole), rest)
            holding[i] = holding[i] + addition
            rest = rest - addition
    return np.array(holding)


def gaussian(stream_key, shape, scale, limit, kind=jnp.bfloat16):
    drawn = jax.random.normal(stream_key, shape, jnp.float32) * scale
    return jnp.minimum(jnp.maximum(drawn, -limit), limit).astype(kind)


def setup_inputs(seed: int = 0) -> dict:
    arg_keys = jax.random.split(jax.random.key(seed), 15)
    tile_pixels = draw_tile_pixels(jax.random.fold_in(arg_keys[14], 71), 0)
    owner_keys = jax.random.split(jax.random.fold_in(arg_keys[1], 1), PARCELS // PAR_DEV)
    owner_turns = jax.random.permutation(jax.random.fold_in(arg_keys[1], 3), PARCELS // PAR_DEV)
    owner = jax.vmap(lambda own, number: routed_block(jax.random.fold_in(arg_keys[1], 2), own, number, PAR_DEV, N_PARCEL, 1, CAP, 2))(owner_keys, owner_turns).reshape((PARCELS, 1))
    pix_count = touch_ends(jax.random.randint(arg_keys[2], (PARCELS,), 1, S + 1), jax.random.fold_in(arg_keys[2], 1), 1, S).astype(jnp.int32)
    cloud = touch_ends((jax.random.randint(arg_keys[3], (PARCELS, DATES), 0, 3) < 1).astype(jnp.int32), jax.random.fold_in(arg_keys[3], 1), 0, 1)
    w_pix1 = gaussian(arg_keys[4], (C, HP), C ** -0.5, 2.0)
    w_pix2 = gaussian(arg_keys[5], (HP, HP), HP ** -0.5, 0.5)
    w_embed = draw_w_embed(jax.random.fold_in(arg_keys[14], 71), 0)
    norm_gain = jnp.clip(1.0 + 0.1 * jax.random.normal(arg_keys[7], (D,), jnp.float32), 0.5, 1.5).astype(jnp.bfloat16)
    w_qkv = gaussian(arg_keys[8], (D, 3 * D), D ** -0.5, 0.1875)
    w_out = gaussian(arg_keys[9], (D, D), D ** -0.5, 0.1875)
    head_scale = jnp.clip(jnp.exp(jax.random.uniform(arg_keys[10], (H,), jnp.float32, math.log(2.0), math.log(30.0))), 2.0, 30.0)
    logit_scale = jnp.clip(jnp.exp(jax.random.uniform(arg_keys[11], (1,), jnp.float32, math.log(5.0), math.log(30.0))), 5.0, 30.0)
    pos_ids = touch_ends(jax.random.randint(arg_keys[12], (PARCELS,), 0, GROUP), jax.random.fold_in(arg_keys[12], 1), 0, GROUP - 1).astype(jnp.int32)
    neg_ids = touch_ends(jax.random.randint(arg_keys[13], (PARCELS, NNEG), 0, GROUP), jax.random.fold_in(arg_keys[13], 1), 0, GROUP - 1).astype(jnp.int32)
    return dict(tile_pixels=tile_pixels, owner=owner, pix_count=pix_count, cloud=cloud, w_pix1=w_pix1, w_pix2=w_pix2, w_embed=w_embed, norm_gain=norm_gain, w_qkv=w_qkv, w_out=w_out, head_scale=head_scale, logit_scale=logit_scale, pos_ids=pos_ids, neg_ids=neg_ids)


def slot_ranks(block_owner, tile_count):
    tiles = jnp.arange(tile_count, dtype=jnp.int32)
    onehot = (block_owner[..., None] == tiles).astype(jnp.int32)
    before = jnp.cumsum(onehot, axis=-2) - onehot
    return lax.optimization_barrier(jnp.sum(before * onehot, axis=-1)).astype(jnp.int32)

def pool_pixels(pixels, counts, w_pix1, w_pix2):
    channels = w_pix1.shape[0]
    row_count = pixels.shape[0]
    pix_width = pixels.shape[1] // channels
    flattened = pixels.reshape(row_count * pix_width, channels)
    hidden_one = jax.nn.relu(jnp.dot(flattened, w_pix1, preferred_element_type=jnp.float32)).astype(jnp.bfloat16)
    hidden_two = jax.nn.relu(jnp.dot(hidden_one, w_pix2, preferred_element_type=jnp.float32))
    hidden_two = hidden_two.reshape(row_count, pix_width, -1)
    valid_mask = (jnp.arange(pix_width, dtype=jnp.int32)[None, :] < counts[:, None]).astype(jnp.float32)
    number = jnp.maximum(counts, 1).astype(jnp.float32)[:, None]
    center = lax.optimization_barrier(jnp.sum(hidden_two * valid_mask[:, :, None], axis=1)) / number
    spread = lax.optimization_barrier(jnp.sum(valid_mask[:, :, None] * (hidden_two - center[:, None, :]) ** 2, axis=1)) / number
    deviation = jnp.sqrt(jnp.maximum(spread, 0.01))
    return jnp.concatenate([center, deviation], axis=-1).astype(jnp.bfloat16)

def date_code(date_total, model_width):
    steps_t = jnp.arange(date_total, dtype=jnp.float32)[:, None]
    pair_index = jnp.arange(model_width // 2, dtype=jnp.float32)[None, :]
    angles = steps_t * jnp.exp(-2.0 * pair_index / model_width * jnp.log(10000.0))
    return jnp.stack([jnp.sin(angles), jnp.cos(angles)], axis=-1).reshape(date_total, model_width)

def unit_rows(vectors):
    return vectors * lax.rsqrt(lax.optimization_barrier(jnp.sum(vectors * vectors, axis=-1, keepdims=True)) + 1e-06)

def attend(tokens, cloudy, norm_gain, w_qkv, w_out, head_scale):
    date_total, parcels, model_width = tokens.shape
    head_count = head_scale.shape[0]
    date_state = tokens.astype(jnp.float32) + date_code(date_total, model_width)[:, None, :]
    center = lax.optimization_barrier(jnp.mean(date_state, axis=-1, keepdims=True))
    spread = lax.optimization_barrier(jnp.mean((date_state - center) ** 2, axis=-1, keepdims=True))
    normed = ((date_state - center) * lax.rsqrt(spread + 1e-05) * norm_gain.astype(jnp.float32)).astype(jnp.bfloat16)
    packed = jnp.dot(normed.reshape(-1, model_width), w_qkv, preferred_element_type=jnp.float32)
    packed = packed.reshape(date_total, parcels, 3, head_count, model_width // head_count)
    queries = unit_rows(packed[:, :, 0])
    key_unit = unit_rows(packed[:, :, 1])
    values = packed[:, :, 2]
    scores = jnp.einsum('qphd,kphd->phqk', queries, key_unit) * head_scale.astype(jnp.float32)[None, :, None, None]
    clear_dates = cloudy == 0
    diagonal_mask = jnp.arange(date_total)[:, None] == jnp.arange(date_total)[None, :]
    allowed = clear_dates[:, None, :] | diagonal_mask[None, :, :]
    scores = jnp.where(allowed[:, None, :, :], scores, -1000000000.0)
    weights = jax.nn.softmax(scores, axis=-1)
    mixed_heads = jnp.einsum('phqk,kphd->qphd', weights, values).reshape(-1, model_width).astype(jnp.bfloat16)
    update = jnp.dot(mixed_heads, w_out, preferred_element_type=jnp.float32).reshape(date_total, parcels, model_width)
    return lax.optimization_barrier(jnp.mean(date_state + update, axis=0)).astype(jnp.bfloat16)

def contrast(similarity, pos_ids, neg_ids, logit_scale):
    positive = jnp.take_along_axis(similarity, pos_ids[:, None], axis=1) * logit_scale[0]
    negative = jnp.take_along_axis(similarity, neg_ids, axis=1) * logit_scale[0]
    logits = jnp.concatenate([positive, negative], axis=1)
    return jax.nn.logsumexp(logits, axis=1) - positive[:, 0]

def reference(tile_pixels, owner, pix_count, cloud, w_pix1, w_pix2, w_embed, norm_gain, w_qkv, w_out, head_scale, logit_scale, pos_ids, neg_ids):
    tile_owner = owner[:, 0].reshape(N_PARCEL, PAR_DEV)
    slot_rank = slot_ranks(tile_owner, N_PARCEL)
    target = jnp.arange(N_PARCEL, dtype=jnp.int32)[:, None]
    row_index = ((tile_owner * N_PARCEL + target) * CAP + slot_rank).reshape(-1).astype(jnp.int32)
    picked = jnp.take(tile_pixels, row_index, axis=1)

    def encode_date(one_date):
        pooled = pool_pixels(one_date, pix_count, w_pix1, w_pix2)
        return jnp.dot(pooled, w_embed, preferred_element_type=jnp.float32).astype(jnp.bfloat16)
    encoded = lax.map(encode_date, picked)
    blocks = jnp.moveaxis(encoded.reshape(DATES, N_PARCEL, PAR_DEV, D), 1, 0)
    cloud_blocks = cloud.reshape(N_PARCEL, PAR_DEV, DATES)

    def attend_block(block_pair):
        return attend(block_pair[0], block_pair[1], norm_gain, w_qkv, w_out, head_scale)
    embedding = lax.map(attend_block, (blocks, cloud_blocks)).reshape(PARCELS, D)
    group_rows = PAR_DEV // N_DATE
    grouped = jnp.moveaxis(embedding.reshape(N_PARCEL, N_DATE, group_rows, D), 1, 0).reshape(N_DATE, GROUP, D)
    unit_group = unit_rows(grouped.astype(jnp.float32))
    similarity = jnp.einsum('gad,gbd->gab', unit_group, unit_group, precision=lax.Precision.HIGHEST)
    pos_group = jnp.moveaxis(pos_ids.reshape(N_PARCEL, N_DATE, group_rows), 1, 0).reshape(N_DATE, GROUP)
    neg_group = jnp.moveaxis(neg_ids.reshape(N_PARCEL, N_DATE, group_rows, NNEG), 1, 0).reshape(N_DATE, GROUP, NNEG)
    losses = jax.vmap(contrast, in_axes=(0, 0, 0, None))(similarity, pos_group, neg_group, logit_scale)
    contrast_loss = jnp.moveaxis(losses.reshape(N_DATE, N_PARCEL, group_rows), 0, 1).reshape(PARCELS)
    return (embedding, contrast_loss)
```

```python
import jax
import jax.numpy as jnp
import numpy as np
from jax import lax
from jax.experimental import pallas as pl
from jax.experimental.pallas import tpu as pltpu
from jax.sharding import PartitionSpec as P

PAR_DEV = 64
CAP = 4
SETS = 64
BF = jnp.bfloat16
F32 = jnp.float32
I32 = jnp.int32
LOG2E = 1.4426950408889634


def iota(shape, dim):
    return lax.broadcasted_iota(I32, shape, dim)


def mm(left, right):
    return jnp.dot(left, right, preferred_element_type=F32)


def mm_nt(left, right):
    return lax.dot_general(left, right, (((1,), (1,)), ((), ())), preferred_element_type=F32)


def rep(block, times):
    return jnp.concatenate([block] * times, axis=0)


def pool_kernel(tile_ref, x_ref, own_ref, cnt_ref, w1_ref, w2_ref, out_ref, w1s, ps):
    rows = 4 * 128
    match = own_ref[...] == tile_ref[0]
    li = iota((128, 128), 0)
    lj = iota((128, 128), 1)
    before = ((li < lj) & ((li // 64) == (lj // 64))).astype(BF)
    rank = mm(match.astype(F32).astype(BF), before)
    code = jnp.where(match, rank.astype(I32), -1)
    sub = iota((16, 8, 128), 1)
    lane = iota((16, 8, 128), 2)
    hit = (code[:, None, :] == (sub % 4)) & ((lane // 64) == (sub // 4))
    amount = jnp.where(hit, cnt_ref[...][:, None, :], 0).reshape(128, 128)
    counts = mm(amount.astype(F32).astype(BF), jnp.ones((128, 128), BF))

    channel = (iota((640, 16), 0) % 10 == iota((640, 16), 1)).astype(BF)
    w1 = jnp.concatenate([w1_ref[...].astype(F32), jnp.zeros((6, 128), F32)], axis=0)
    tiled = mm(channel, w1.astype(BF))
    windows = []
    for j in range(SETS // 2):
        low = 20 * j
        start = low // 128 * 128
        depth = 256 if low + 20 > start + 128 else 128
        windows.append((start, depth))
        part = tiled[start : start + depth]
        row = iota((depth, 128), 0) + start
        w1s[j, 0:depth, 0:128] = jnp.where((row >= low) & (row < low + 10), part, 0.0).astype(BF)
        w1s[j, 0:depth, 128:256] = jnp.where(
            (row >= low + 10) & (row < low + 20), part, 0.0
        ).astype(BF)
    zero = jnp.zeros((128, 128), BF)
    w2 = w2_ref[...]
    w2 = jnp.concatenate(
        [jnp.concatenate([w2, zero], axis=1), jnp.concatenate([zero, w2], axis=1)], axis=0
    )

    x = x_ref[...].reshape(rows, 640)
    valid = (iota((128, 640), 1) // 10).astype(F32) < jnp.concatenate([counts] * 5, axis=1)
    to_all = ((iota((128, 640), 1) % 10) == iota((128, 640), 0)).astype(BF)
    first = mm(x[:, 0:128], to_all)
    ps[...] = jnp.where(rep(valid, 4), x.astype(F32), first).astype(BF)
    origin = total = square = None
    for j, (start, depth) in enumerate(windows):
        hidden = mm(ps[:, start : start + depth], w1s[j, 0:depth, :])
        hidden = jnp.maximum(hidden.astype(BF), 0)
        hidden = jnp.maximum(mm(hidden, w2), 0.0)
        if j == 0:
            origin = hidden[:, 0:128]
            total = hidden[:, 128:256] - origin
            square = total * total
        else:
            even = hidden[:, 0:128] - origin
            odd = hidden[:, 128:256] - origin
            total = total + (even + odd)
            square = square + (even * even + odd * odd)
    number = jnp.maximum(rep(counts, 4), 1.0)
    shift = total / number
    deviation = jnp.sqrt(jnp.maximum(square / number - shift * shift, 0.01))
    pooled = jnp.concatenate([origin + shift, deviation], axis=1).astype(BF)
    po = iota((256, 256), 0)
    pi = iota((256, 256), 1)
    order = ((po // 16 == pi // 4 % 16) & (po // 4 % 4 == pi // 64) & (po % 4 == pi % 4)).astype(BF)
    for half in range(2):
        part = jnp.concatenate(
            [pooled[d * 128 + half * 64 : d * 128 + half * 64 + 64] for d in range(4)], axis=0
        )
        out_ref[half * 16 : half * 16 + 16] = mm(order, part).astype(BF).reshape(16, 16, 256)


def pool_slots(tile, pixels, owner, counts, w_pix1, w_pix2):
    vmem = pl.BlockSpec(memory_space=pltpu.VMEM)
    return pl.pallas_call(
        pool_kernel,
        out_shape=jax.ShapeDtypeStruct((32, 16, 256), BF),
        in_specs=[pl.BlockSpec(memory_space=pltpu.SMEM)] + [vmem] * 5,
        out_specs=vmem,
        scratch_shapes=[pltpu.VMEM((32, 256, 256), BF), pltpu.VMEM((512, 640), BF)],
        compiler_params=pltpu.CompilerParams(vmem_limit_bytes=40 << 20),
        name="pool_slots",
    )(tile, pixels, owner, counts, w_pix1, w_pix2)


def attend_kernel(
    tok_ref, clear_ref, code_ref, gain_ref, scale_ref, we_ref, wqkv_ref, wo_ref, emb_ref, all_ref
):
    encoded = mm(tok_ref[...], we_ref[...]).astype(BF).astype(F32)
    code = jnp.broadcast_to(code_ref[...][:, None, :], (32, 8, 1024)).reshape(256, 1024)
    state = encoded + code
    state_mean = jnp.mean(state.reshape(32, 8, 1024), axis=0)
    center = jnp.mean(state, axis=1, keepdims=True)
    moved = state - center
    spread = jnp.mean(moved * moved, axis=1, keepdims=True)
    normed = (moved * lax.rsqrt(spread + 1e-05) * gain_ref[...].astype(F32)).astype(BF)

    seg = (iota((256, 256), 0) // 64 == iota((256, 256), 1) // 64).astype(BF)
    qi = iota((256, 256), 0)
    ki = iota((256, 256), 1)
    mask = jnp.where(
        (qi % 8 == ki % 8) & ((qi == ki) | (clear_ref[...] > 0.0)), jnp.float32(1), jnp.float32(0)
    )
    left = iota((256, 128), 1) < 64
    ones = jnp.ones((256, 128), BF)
    none = jnp.zeros((256, 128), BF)
    means = []
    for c in range(4):
        span = slice(256 * c, 256 * c + 256)
        queries = mm(normed, wqkv_ref[:, 256 * c : 256 * c + 256])
        keys = mm(normed, wqkv_ref[:, 1024 + 256 * c : 1024 + 256 * c + 256])
        values = mm(normed, wqkv_ref[:, 2048 + 256 * c : 2048 + 256 * c + 256]).astype(BF)
        q_sum = mm((queries * queries).astype(BF), seg)
        k_sum = mm((keys * keys).astype(BF), seg)
        queries = (queries * (lax.rsqrt(q_sum + 1e-06) * (scale_ref[:, span] * LOG2E))).astype(BF)
        keys = (keys * lax.rsqrt(k_sum + 1e-06)).astype(BF)
        for pair in range(2):
            lanes = slice(128 * pair, 128 * pair + 128)
            q_pair = queries[:, lanes]
            k_pair = keys[:, lanes]
            right = jnp.concatenate([values[:, lanes], ones], axis=1)
            mixed = []
            for side in range(2):
                k_side = jnp.where(left, k_pair, none) if side == 0 else jnp.where(left, none, k_pair)
                weights = (jnp.exp2(mm_nt(q_pair, k_side)) * mask).astype(BF)
                both = mm(weights, right)
                mixed.append(both[:, 0:128] / both[:, 128:256])
            means.append(jnp.mean(jnp.where(left, mixed[0], mixed[1]).reshape(32, 8, 128), axis=0))
    mean = jnp.concatenate(means, axis=1)
    high = mean.astype(BF)
    low = (mean - high.astype(F32)).astype(BF)
    update = mm(jnp.concatenate([high, low], axis=0), wo_ref[...])
    embedding = (state_mean + (update[0:8] + update[8:16])).astype(BF)
    emb_ref[...] = embedding
    all_ref[...] = jnp.broadcast_to(embedding[None], (32, 8, 1024))


def attend(tokens, clear, code, gain, scale, w_embed, w_qkv, w_out):
    vmem = pl.BlockSpec(memory_space=pltpu.VMEM)
    return pl.pallas_call(
        attend_kernel,
        out_shape=(
            jax.ShapeDtypeStruct((8, 1024), BF),
            jax.ShapeDtypeStruct((32, 8, 1024), BF),
        ),
        in_specs=[vmem] * 8,
        out_specs=(vmem, vmem),
        compiler_params=pltpu.CompilerParams(vmem_limit_bytes=40 << 20),
        name="attend",
    )(tokens, clear, code, gain, scale, w_embed, w_qkv, w_out)


def contrast_kernel(scale_ref, emb_ref, all_ref, pos_ref, neg_ref, out_ref):
    others = all_ref[...].astype(F32)
    square = others * others
    high = square.astype(BF)
    low = (square - high.astype(F32)).astype(BF)
    ones = jnp.ones((8, 1024), BF)
    other_sum = mm_nt(ones, high) + mm_nt(ones, low)
    anchors = emb_ref[...].astype(F32)
    own_sum = jnp.sum(anchors * anchors, axis=1, keepdims=True)
    similarity = mm_nt(emb_ref[...], all_ref[...])
    similarity = similarity * lax.rsqrt(own_sum + 1e-06) * lax.rsqrt(other_sum + 1e-06)
    logits = similarity * scale_ref[0]
    member = iota((8, 256), 1)
    positive = jnp.sum(jnp.where(member == pos_ref[...], logits, 0.0), axis=1, keepdims=True)
    ids = neg_ref[...]
    within = ids % 128
    near = jnp.take_along_axis(logits[:, 0:128], within, axis=1)
    far = jnp.take_along_axis(logits[:, 128:256], within, axis=1)
    negative = jnp.where(ids < 128, near, far)
    loss = jnp.log(1.0 + jnp.sum(jnp.exp(negative - positive), axis=1, keepdims=True))
    diagonal = iota((8, 128), 0) == iota((8, 128), 1)
    out_ref[...] = jnp.sum(jnp.where(diagonal, loss, 0.0), axis=0, keepdims=True)[:, 0:8]


def contrast(scale, embedding, others, pos_ids, neg_ids):
    vmem = pl.BlockSpec(memory_space=pltpu.VMEM)
    return pl.pallas_call(
        contrast_kernel,
        out_shape=jax.ShapeDtypeStruct((1, 8), F32),
        in_specs=[pl.BlockSpec(memory_space=pltpu.SMEM)] + [vmem] * 4,
        out_specs=vmem,
        compiler_params=pltpu.CompilerParams(vmem_limit_bytes=16 << 20),
        name="contrast",
    )(scale, embedding, others, pos_ids, neg_ids)


def date_code(dates, width):
    steps = np.arange(dates, dtype=np.float64)[:, None]
    pair = np.arange(width // 2, dtype=np.float64)[None, :]
    angles = steps * np.exp(-2.0 * pair / width * np.log(10000.0))
    table = np.stack([np.sin(angles), np.cos(angles)], axis=-1).reshape(dates, width)
    return table.astype(np.float32)


def slot_matrix(block_owner):
    place = jnp.arange(PAR_DEV, dtype=I32)
    same = (block_owner[:, None] == block_owner[None, :]) & (place[None, :] < place[:, None])
    rank = jnp.sum(same.astype(I32), axis=1)
    source = (block_owner * 16 + rank).reshape(8, 1, 8) + 4 * jnp.arange(4, dtype=I32)[None, :, None]
    return (source.reshape(256, 1) == jnp.arange(512, dtype=I32)[None, :]).astype(BF)


def per_device(
    tile_pixels,
    owner,
    pix_count,
    cloud,
    w_pix1,
    w_pix2,
    w_embed,
    norm_gain,
    w_qkv,
    w_out,
    head_scale,
    logit_scale,
    pos_ids,
    neg_ids,
):
    block = lax.axis_index("parcel")
    pooled = pool_slots(
        block.reshape(1).astype(I32),
        tile_pixels,
        owner.reshape(16, 128),
        pix_count.reshape(16, 128),
        w_pix1,
        w_pix2,
    )
    arrived = lax.all_to_all(pooled, "parcel", split_axis=0, concat_axis=0, tiled=True)
    pick = slot_matrix(lax.dynamic_slice_in_dim(owner[:, 0], block * PAR_DEV, PAR_DEV))
    moving = mm(pick, arrived.reshape(512, 256)).astype(BF).reshape(8, 32, 256)
    tokens = lax.all_to_all(moving, "date", split_axis=0, concat_axis=0, tiled=True)
    embedding, copies = attend(
        tokens.reshape(256, 256),
        (cloud.T == 0).astype(F32).reshape(1, 256),
        jnp.asarray(date_code(32, 1024)),
        norm_gain.reshape(1, 1024),
        jnp.repeat(head_scale, 64).reshape(1, 1024),
        w_embed,
        w_qkv,
        w_out,
    )
    others = lax.all_to_all(copies, "parcel", split_axis=0, concat_axis=0, tiled=True)
    loss = contrast(
        logit_scale, embedding, others.reshape(256, 1024), pos_ids.reshape(8, 1), neg_ids
    )
    return (embedding, loss.reshape(8))


def solution(mesh):
    in_specs = (
        P("date", "parcel", None),
        P(),
        P(),
        P(("parcel", "date"), None),
        P(),
        P(),
        P(),
        P(),
        P(),
        P(),
        P(),
        P(),
        P(("parcel", "date")),
        P(("parcel", "date"), None),
    )
    out_specs = (P(("parcel", "date"), None), P(("parcel", "date")))
    return jax.shard_map(
        per_device, mesh=mesh, in_specs=in_specs, out_specs=out_specs, check_vma=False
    )
```

```python
import jax
import jax.numpy as jnp
import numpy as np
from jax import lax
from jax.experimental import pallas as pl
from jax.experimental.pallas import tpu as pltpu
from jax.sharding import PartitionSpec as P

PAR_DEV = 64
CAP = 4
SETS = 64
BF = jnp.bfloat16
F32 = jnp.float32
I32 = jnp.int32
LOG2E = 1.4426950408889634


def iota(shape, dim):
    return lax.broadcasted_iota(I32, shape, dim)


def mm(left, right):
    return jnp.dot(left, right, preferred_element_type=F32)


def mm_nt(left, right):
    return lax.dot_general(left, right, (((1,), (1,)), ((), ())), preferred_element_type=F32)


def rep(block, times):
    return jnp.concatenate([block] * times, axis=0)


def pool_kernel(
    tile_ref, x_any, own_any, cnt_any, w1_any, w2_any, out_ref,
    x_ref, own_ref, cnt_ref, w1_ref, w2_ref, w1s, ps, sems,
):
    pairs = [(own_any, own_ref), (cnt_any, cnt_ref), (w1_any, w1_ref), (w2_any, w2_ref), (x_any, x_ref)]
    copies = [pltpu.make_async_copy(a, b, sems.at[i]) for i, (a, b) in enumerate(pairs)]
    for copy in copies:
        copy.start()
    copies[0].wait()
    copies[1].wait()
    rows = 4 * 128
    match = own_ref[...] == tile_ref[0]
    li = iota((128, 128), 0)
    lj = iota((128, 128), 1)
    before = ((li < lj) & ((li // 64) == (lj // 64))).astype(BF)
    rank = mm(match.astype(F32).astype(BF), before)
    code = jnp.where(match, rank.astype(I32), -1)
    sub = iota((16, 8, 128), 1)
    lane = iota((16, 8, 128), 2)
    hit = (code[:, None, :] == (sub % 4)) & ((lane // 64) == (sub // 4))
    amount = jnp.where(hit, cnt_ref[...][:, None, :], 0).reshape(128, 128)
    counts = mm(amount.astype(F32).astype(BF), jnp.ones((128, 128), BF))

    copies[2].wait()
    channel = (iota((640, 16), 0) % 10 == iota((640, 16), 1)).astype(BF)
    w1 = jnp.concatenate([w1_ref[...].astype(F32), jnp.zeros((6, 128), F32)], axis=0)
    tiled = mm(channel, w1.astype(BF))
    windows = []
    for j in range(SETS // 2):
        low = 20 * j
        start = low // 128 * 128
        depth = 256 if low + 20 > start + 128 else 128
        windows.append((start, depth))
        part = tiled[start : start + depth]
        row = iota((depth, 128), 0) + start
        w1s[j, 0:depth, 0:128] = jnp.where((row >= low) & (row < low + 10), part, 0.0).astype(BF)
        w1s[j, 0:depth, 128:256] = jnp.where(
            (row >= low + 10) & (row < low + 20), part, 0.0
        ).astype(BF)
    zero = jnp.zeros((128, 128), BF)
    copies[3].wait()
    w2 = w2_ref[...]
    w2 = jnp.concatenate(
        [jnp.concatenate([w2, zero], axis=1), jnp.concatenate([zero, w2], axis=1)], axis=0
    )

    copies[4].wait()
    x = x_ref[...].reshape(rows, 640)
    valid = (iota((128, 640), 1) // 10).astype(F32) < jnp.concatenate([counts] * 5, axis=1)
    to_all = ((iota((128, 640), 1) % 10) == iota((128, 640), 0)).astype(BF)
    first = mm(x[:, 0:128], to_all)
    ps[...] = jnp.where(rep(valid, 4), x.astype(F32), first).astype(BF)
    origin = total = square = None
    for j, (start, depth) in enumerate(windows):
        hidden = mm(ps[:, start : start + depth], w1s[j, 0:depth, :])
        hidden = jnp.maximum(hidden.astype(BF), 0)
        hidden = jnp.maximum(mm(hidden, w2), 0.0)
        if j == 0:
            origin = hidden[:, 0:128]
            total = hidden[:, 128:256] - origin
            square = total * total
        else:
            even = hidden[:, 0:128] - origin
            odd = hidden[:, 128:256] - origin
            total = total + (even + odd)
            square = square + (even * even + odd * odd)
    number = jnp.maximum(rep(counts, 4), 1.0)
    shift = total / number
    deviation = jnp.sqrt(jnp.maximum(square / number - shift * shift, 0.01))
    pooled = jnp.concatenate([origin + shift, deviation], axis=1).astype(BF)
    po = iota((256, 256), 0)
    pi = iota((256, 256), 1)
    order = ((po // 16 == pi // 4 % 16) & (po // 4 % 4 == pi // 64) & (po % 4 == pi % 4)).astype(BF)
    for half in range(2):
        part = jnp.concatenate(
            [pooled[d * 128 + half * 64 : d * 128 + half * 64 + 64] for d in range(4)], axis=0
        )
        out_ref[half * 16 : half * 16 + 16] = mm(order, part).astype(BF).reshape(16, 16, 256)


def pool_slots(tile, pixels, owner, counts, w_pix1, w_pix2):
    return pl.pallas_call(
        pool_kernel,
        out_shape=jax.ShapeDtypeStruct((32, 16, 256), BF),
        in_specs=[pl.BlockSpec(memory_space=pltpu.SMEM)] + [pl.BlockSpec(memory_space=pl.ANY)] * 5,
        out_specs=pl.BlockSpec(memory_space=pltpu.VMEM),
        scratch_shapes=[
            pltpu.VMEM((4, 128, 640), BF),
            pltpu.VMEM((16, 128), I32),
            pltpu.VMEM((16, 128), I32),
            pltpu.VMEM((10, 128), BF),
            pltpu.VMEM((128, 128), BF),
            pltpu.VMEM((32, 256, 256), BF),
            pltpu.VMEM((512, 640), BF),
            pltpu.SemaphoreType.DMA((5,)),
        ],
        compiler_params=pltpu.CompilerParams(vmem_limit_bytes=60 << 20),
        name="pool_slots",
    )(tile, pixels, owner, counts, w_pix1, w_pix2)


def prepare_kernel(
    block_ref, after, own_any, cloud_any, code_any, we_any,
    pick_ref, mask_ref, code_ref, we_ref, own_ref, cloud_ref, sems,
):
    pairs = [
        (own_any, own_ref),
        (cloud_any, cloud_ref),
        (we_any, we_ref),
        (code_any, code_ref),
    ]
    copies = [pltpu.make_async_copy(a, b, sems.at[i]) for i, (a, b) in enumerate(pairs)]
    for copy in copies:
        copy.start()
    copies[0].wait()
    copies[1].wait()
    block = block_ref[0]
    owner = own_ref[pl.ds(block // 2, 1), :].astype(F32)
    sub = iota((128, 128), 0)
    lane = iota((128, 128), 1)
    column = jnp.sum(jnp.where(sub == lane, owner, 0.0), axis=1, keepdims=True)
    earlier = (column == owner) & (sub < lane) & (sub // 64 == lane // 64)
    rank = jnp.sum(jnp.where(earlier, 1.0, 0.0), axis=0, keepdims=True)
    source = owner * 16.0 + rank
    row = iota((256, 128), 0)
    parcel = (block % 2) * 64 + row // 32 * 8 + row % 8
    wanted = jnp.sum(jnp.where(iota((256, 128), 1) == parcel, source, 0.0), axis=1, keepdims=True)
    wanted = wanted.astype(I32) + iota((256, 1), 0) // 8 % 4 * 4
    pick_ref[...] = jnp.where(iota((256, 512), 1) == wanted, 1.0, 0.0).astype(BF)
    dates = (iota((32, 256), 1) // 8 == iota((32, 256), 0)).astype(BF)
    clouds = mm(cloud_ref[...].astype(F32).astype(BF), dates)
    own_row = iota((8, 256), 0) == iota((8, 256), 1) % 8
    cloudy = jnp.sum(jnp.where(own_row, clouds, 0.0), axis=0, keepdims=True)
    qi = iota((256, 256), 0)
    ki = iota((256, 256), 1)
    mask_ref[...] = jnp.where((qi % 8 == ki % 8) & ((qi == ki) | (cloudy == 0.0)), 1.0, 0.0)
    for copy in copies[2:]:
        copy.wait()


def prepare(block, after, owner, cloud, code, w_embed):
    kept = (code, w_embed)
    return pl.pallas_call(
        prepare_kernel,
        out_shape=(
            jax.ShapeDtypeStruct((256, 512), BF),
            jax.ShapeDtypeStruct((256, 256), F32),
        )
        + tuple(jax.ShapeDtypeStruct(a.shape, a.dtype) for a in kept),
        in_specs=[pl.BlockSpec(memory_space=pltpu.SMEM)] + [pl.BlockSpec(memory_space=pl.ANY)] * 5,
        out_specs=(pl.BlockSpec(memory_space=pltpu.VMEM),) * 4,
        scratch_shapes=[
            pltpu.VMEM((16, 128), I32),
            pltpu.VMEM((8, 32), I32),
            pltpu.SemaphoreType.DMA((4,)),
        ],
        compiler_params=pltpu.CompilerParams(vmem_limit_bytes=48 << 20),
        cost_estimate=pl.CostEstimate(flops=0, bytes_accessed=8 << 20, transcendentals=0),
        name="prepare",
    )(block, after, owner, cloud, *kept)


def attend_kernel(
    scale_ref, tok_ref, mask_ref, code_ref, gain_ref, we_ref, wqkv_any, wo_any,
    emb_ref, all_ref, wqkv_ref, wo_ref, sems,
):
    copies = []
    for c in range(4):
        for part in range(3):
            columns = pl.ds(1024 * part + 256 * c, 256)
            copies.append(
                pltpu.make_async_copy(
                    wqkv_any.at[:, columns], wqkv_ref.at[:, columns], sems.at[3 * c + part]
                )
            )
    copies.append(pltpu.make_async_copy(wo_any, wo_ref, sems.at[12]))
    for copy in copies:
        copy.start()
    encoded = mm(tok_ref[...], we_ref[...]).astype(BF).astype(F32)
    code = jnp.broadcast_to(code_ref[...][:, None, :], (32, 8, 1024)).reshape(256, 1024)
    state = encoded + code
    state_mean = jnp.mean(state.reshape(32, 8, 1024), axis=0)
    center = jnp.mean(state, axis=1, keepdims=True)
    moved = state - center
    spread = jnp.mean(moved * moved, axis=1, keepdims=True)
    normed = (moved * lax.rsqrt(spread + 1e-05) * gain_ref[...].astype(F32)).astype(BF)

    seg = (iota((256, 256), 0) // 64 == iota((256, 256), 1) // 64).astype(BF)
    mask = mask_ref[...]
    head = iota((1, 256), 1) // 64
    left = iota((256, 128), 1) < 64
    ones = jnp.ones((256, 128), BF)
    none = jnp.zeros((256, 128), BF)
    means = []
    for c in range(4):
        scale = jnp.zeros((1, 256), F32)
        for i in range(4):
            scale = jnp.where(head == i, scale_ref[4 * c + i] * LOG2E, scale)
        copies[3 * c].wait()
        queries = mm(normed, wqkv_ref[:, 256 * c : 256 * c + 256])
        copies[3 * c + 1].wait()
        keys = mm(normed, wqkv_ref[:, 1024 + 256 * c : 1024 + 256 * c + 256])
        copies[3 * c + 2].wait()
        values = mm(normed, wqkv_ref[:, 2048 + 256 * c : 2048 + 256 * c + 256]).astype(BF)
        q_sum = mm((queries * queries).astype(BF), seg)
        k_sum = mm((keys * keys).astype(BF), seg)
        queries = (queries * (lax.rsqrt(q_sum + 1e-06) * scale)).astype(BF)
        keys = (keys * lax.rsqrt(k_sum + 1e-06)).astype(BF)
        for pair in range(2):
            lanes = slice(128 * pair, 128 * pair + 128)
            q_pair = queries[:, lanes]
            k_pair = keys[:, lanes]
            right = jnp.concatenate([values[:, lanes], ones], axis=1)
            mixed = []
            for side in range(2):
                k_side = jnp.where(left, k_pair, none) if side == 0 else jnp.where(left, none, k_pair)
                weights = (jnp.exp2(mm_nt(q_pair, k_side)) * mask).astype(BF)
                both = mm(weights, right)
                mixed.append(both[:, 0:128] / both[:, 128:256])
            means.append(jnp.mean(jnp.where(left, mixed[0], mixed[1]).reshape(32, 8, 128), axis=0))
    mean = jnp.concatenate(means, axis=1)
    high = mean.astype(BF)
    low = (mean - high.astype(F32)).astype(BF)
    copies[12].wait()
    update = mm(jnp.concatenate([high, low], axis=0), wo_ref[...])
    embedding = (state_mean + (update[0:8] + update[8:16])).astype(BF)
    emb_ref[...] = embedding
    all_ref[...] = jnp.broadcast_to(embedding[None], (32, 8, 1024))


def attend(scale, tokens, mask, code, gain, w_embed, w_qkv, w_out):
    vmem = pl.BlockSpec(memory_space=pltpu.VMEM)
    return pl.pallas_call(
        attend_kernel,
        out_shape=(
            jax.ShapeDtypeStruct((8, 1024), BF),
            jax.ShapeDtypeStruct((32, 8, 1024), BF),
        ),
        in_specs=[pl.BlockSpec(memory_space=pltpu.SMEM)]
        + [vmem] * 5
        + [pl.BlockSpec(memory_space=pl.ANY)] * 2,
        out_specs=(vmem, vmem),
        scratch_shapes=[
            pltpu.VMEM((1024, 3072), BF),
            pltpu.VMEM((1024, 1024), BF),
            pltpu.SemaphoreType.DMA((13,)),
        ],
        compiler_params=pltpu.CompilerParams(vmem_limit_bytes=52 << 20),
        name="attend",
    )(scale, tokens, mask, code, gain, w_embed, w_qkv, w_out)


def contrast_kernel(scale_ref, block_ref, all_ref, pos_ref, neg_ref, out_ref):
    others = all_ref[...].reshape(256, 1024).astype(F32)
    square = others * others
    high = square.astype(BF)
    low = (square - high.astype(F32)).astype(BF)
    ones = jnp.ones((8, 1024), BF)
    other_sum = mm_nt(ones, high) + mm_nt(ones, low)
    mine = all_ref[block_ref[0]]
    anchors = mine.astype(F32)
    own_sum = jnp.sum(anchors * anchors, axis=1, keepdims=True)
    similarity = mm_nt(mine, all_ref[...].reshape(256, 1024))
    similarity = similarity * lax.rsqrt(own_sum + 1e-06) * lax.rsqrt(other_sum + 1e-06)
    logits = similarity * scale_ref[0]
    member = iota((8, 256), 1)
    positive = jnp.sum(jnp.where(member == pos_ref[...], logits, 0.0), axis=1, keepdims=True)
    ids = neg_ref[...]
    within = ids % 128
    near = jnp.take_along_axis(logits[:, 0:128], within, axis=1)
    far = jnp.take_along_axis(logits[:, 128:256], within, axis=1)
    negative = jnp.where(ids < 128, near, far)
    loss = jnp.log(1.0 + jnp.sum(jnp.exp(negative - positive), axis=1, keepdims=True))
    diagonal = iota((8, 128), 0) == iota((8, 128), 1)
    out_ref[...] = jnp.sum(jnp.where(diagonal, loss, 0.0), axis=0, keepdims=True)[:, 0:8]


def contrast(scale, block, others, pos_ids, neg_ids):
    vmem = pl.BlockSpec(memory_space=pltpu.VMEM)
    return pl.pallas_call(
        contrast_kernel,
        out_shape=jax.ShapeDtypeStruct((1, 8), F32),
        in_specs=[pl.BlockSpec(memory_space=pltpu.SMEM)] * 2 + [vmem] * 3,
        out_specs=vmem,
        compiler_params=pltpu.CompilerParams(vmem_limit_bytes=16 << 20),
        name="contrast",
    )(scale, block, others, pos_ids, neg_ids)


def date_code(dates, width):
    steps = np.arange(dates, dtype=np.float64)[:, None]
    pair = np.arange(width // 2, dtype=np.float64)[None, :]
    angles = steps * np.exp(-2.0 * pair / width * np.log(10000.0))
    table = np.stack([np.sin(angles), np.cos(angles)], axis=-1).reshape(dates, width)
    return table.astype(np.float32)


def per_device(
    tile_pixels,
    owner,
    pix_count,
    cloud,
    w_pix1,
    w_pix2,
    w_embed,
    norm_gain,
    w_qkv,
    w_out,
    head_scale,
    logit_scale,
    pos_ids,
    neg_ids,
):
    block = lax.axis_index("parcel").reshape(1).astype(I32)
    owner = owner.reshape(16, 128)
    pooled = pool_slots(
        block, tile_pixels, owner, pix_count.reshape(16, 128), w_pix1, w_pix2
    )
    arrived = lax.all_to_all(pooled, "parcel", split_axis=0, concat_axis=0, tiled=True)
    code = jnp.asarray(date_code(32, 1024))
    pick, mask, code, w_embed = prepare(block, pooled, owner, cloud, code, w_embed)
    moving = mm(pick, arrived.reshape(512, 256)).astype(BF).reshape(8, 32, 256)
    tokens = lax.all_to_all(moving, "date", split_axis=0, concat_axis=0, tiled=True)
    embedding, copies = attend(
        head_scale,
        tokens.reshape(256, 256),
        mask,
        code,
        norm_gain.reshape(1, 1024),
        w_embed,
        w_qkv,
        w_out,
    )
    others = lax.all_to_all(copies, "parcel", split_axis=0, concat_axis=0, tiled=True)
    loss = contrast(logit_scale, block, others, pos_ids.reshape(8, 1), neg_ids)
    return (embedding, loss.reshape(8))


def solution(mesh):
    in_specs = (
        P("date", "parcel", None),
        P(),
        P(),
        P(("parcel", "date"), None),
        P(),
        P(),
        P(),
        P(),
        P(),
        P(),
        P(),
        P(),
        P(("parcel", "date")),
        P(("parcel", "date"), None),
    )
    out_specs = (P(("parcel", "date"), None), P(("parcel", "date")))
    return jax.shard_map(
        per_device, mesh=mesh, in_specs=in_specs, out_specs=out_specs, check_vma=False
    )
```

```python
import jax
import jax.numpy as jnp
import numpy as np
from jax import lax
from jax.experimental import pallas as pl
from jax.experimental.pallas import tpu as pltpu
from jax.sharding import PartitionSpec as P

PAR_DEV = 64
CAP = 4
SETS = 64
BF = jnp.bfloat16
F32 = jnp.float32
I32 = jnp.int32
LOG2E = 1.4426950408889634


def iota(shape, dim):
    return lax.broadcasted_iota(I32, shape, dim)


def mm(left, right):
    return jnp.dot(left, right, preferred_element_type=F32)


def mm_nt(left, right):
    return lax.dot_general(left, right, (((1,), (1,)), ((), ())), preferred_element_type=F32)


def rep(block, times):
    return jnp.concatenate([block] * times, axis=0)


def pool_kernel(
    tile_ref, x_any, own_any, cnt_any, w1_any, w2_any, out_ref,
    x_ref, own_ref, cnt_ref, w1_ref, w2_ref, w1s, ps, sems,
):
    pairs = [(own_any, own_ref), (cnt_any, cnt_ref), (w1_any, w1_ref), (w2_any, w2_ref), (x_any, x_ref)]
    copies = [pltpu.make_async_copy(a, b, sems.at[i]) for i, (a, b) in enumerate(pairs)]
    for copy in copies:
        copy.start()
    copies[0].wait()
    copies[1].wait()
    rows = 4 * 128
    match = own_ref[...] == tile_ref[0]
    li = iota((128, 128), 0)
    lj = iota((128, 128), 1)
    before = ((li < lj) & ((li // 64) == (lj // 64))).astype(BF)
    rank = mm(match.astype(F32).astype(BF), before)
    code = jnp.where(match, rank.astype(I32), -1)
    sub = iota((16, 8, 128), 1)
    lane = iota((16, 8, 128), 2)
    hit = (code[:, None, :] == (sub % 4)) & ((lane // 64) == (sub // 4))
    amount = jnp.where(hit, cnt_ref[...][:, None, :], 0).reshape(128, 128)
    counts = mm(amount.astype(F32).astype(BF), jnp.ones((128, 128), BF))

    copies[2].wait()
    channel = (iota((640, 16), 0) % 10 == iota((640, 16), 1)).astype(BF)
    w1 = jnp.concatenate([w1_ref[...].astype(F32), jnp.zeros((6, 128), F32)], axis=0)
    tiled = mm(channel, w1.astype(BF))
    windows = []
    for j in range(SETS // 2):
        low = 20 * j
        start = low // 128 * 128
        depth = 256 if low + 20 > start + 128 else 128
        windows.append((start, depth))
        part = tiled[start : start + depth]
        row = iota((depth, 128), 0) + start
        w1s[j, 0:depth, 0:128] = jnp.where((row >= low) & (row < low + 10), part, 0.0).astype(BF)
        w1s[j, 0:depth, 128:256] = jnp.where(
            (row >= low + 10) & (row < low + 20), part, 0.0
        ).astype(BF)
    zero = jnp.zeros((128, 128), BF)
    copies[3].wait()
    w2 = w2_ref[...]
    w2 = jnp.concatenate(
        [jnp.concatenate([w2, zero], axis=1), jnp.concatenate([zero, w2], axis=1)], axis=0
    )

    copies[4].wait()
    x = x_ref[...].reshape(rows, 640)
    valid = (iota((128, 640), 1) // 10).astype(F32) < jnp.concatenate([counts] * 5, axis=1)
    to_all = ((iota((128, 640), 1) % 10) == iota((128, 640), 0)).astype(BF)
    first = mm(x[:, 0:128], to_all)
    ps[...] = jnp.where(rep(valid, 4), x.astype(F32), first).astype(BF)
    origin = total = square = None
    for j, (start, depth) in enumerate(windows):
        hidden = mm(ps[:, start : start + depth], w1s[j, 0:depth, :])
        hidden = jnp.maximum(hidden.astype(BF), 0)
        hidden = jnp.maximum(mm(hidden, w2), 0.0)
        if j == 0:
            origin = hidden[:, 0:128]
            total = hidden[:, 128:256] - origin
            square = total * total
        else:
            even = hidden[:, 0:128] - origin
            odd = hidden[:, 128:256] - origin
            total = total + (even + odd)
            square = square + (even * even + odd * odd)
    number = jnp.maximum(rep(counts, 4), 1.0)
    shift = total / number
    deviation = jnp.sqrt(jnp.maximum(square / number - shift * shift, 0.01))
    pooled = jnp.concatenate([origin + shift, deviation], axis=1).astype(BF)
    po = iota((256, 256), 0)
    pi = iota((256, 256), 1)
    order = ((po // 16 == pi // 4 % 16) & (po // 4 % 4 == pi // 64) & (po % 4 == pi % 4)).astype(BF)
    for half in range(2):
        part = jnp.concatenate(
            [pooled[d * 128 + half * 64 : d * 128 + half * 64 + 64] for d in range(4)], axis=0
        )
        out_ref[half * 16 : half * 16 + 16] = mm(order, part).astype(BF).reshape(16, 16, 256)


def pool_slots(tile, pixels, owner, counts, w_pix1, w_pix2):
    return pl.pallas_call(
        pool_kernel,
        out_shape=jax.ShapeDtypeStruct((32, 16, 256), BF),
        in_specs=[pl.BlockSpec(memory_space=pltpu.SMEM)] + [pl.BlockSpec(memory_space=pl.ANY)] * 5,
        out_specs=pl.BlockSpec(memory_space=pltpu.VMEM),
        scratch_shapes=[
            pltpu.VMEM((4, 128, 640), BF),
            pltpu.VMEM((16, 128), I32),
            pltpu.VMEM((16, 128), I32),
            pltpu.VMEM((10, 128), BF),
            pltpu.VMEM((128, 128), BF),
            pltpu.VMEM((32, 256, 256), BF),
            pltpu.VMEM((512, 640), BF),
            pltpu.SemaphoreType.DMA((5,)),
        ],
        compiler_params=pltpu.CompilerParams(vmem_limit_bytes=60 << 20),
        name="pool_slots",
    )(tile, pixels, owner, counts, w_pix1, w_pix2)


def prepare_kernel(
    block_ref, scale_ref, after, own_any, cloud_any, gain_any, code_any, we_any,
    pick_ref, mask_ref, row_ref, code_ref, we_ref, own_ref, cloud_ref, gain_ref, sems,
):
    pairs = [
        (own_any, own_ref),
        (cloud_any, cloud_ref),
        (gain_any, gain_ref),
        (we_any, we_ref),
        (code_any, code_ref),
    ]
    copies = [pltpu.make_async_copy(a, b, sems.at[i]) for i, (a, b) in enumerate(pairs)]
    for copy in copies:
        copy.start()
    copies[0].wait()
    copies[1].wait()
    block = block_ref[0]
    owner = own_ref[pl.ds(block // 2, 1), :].astype(F32)
    sub = iota((128, 128), 0)
    lane = iota((128, 128), 1)
    column = jnp.sum(jnp.where(sub == lane, owner, 0.0), axis=1, keepdims=True)
    earlier = (column == owner) & (sub < lane) & (sub // 64 == lane // 64)
    rank = jnp.sum(jnp.where(earlier, 1.0, 0.0), axis=0, keepdims=True)
    source = owner * 16.0 + rank
    row = iota((256, 128), 0)
    parcel = (block % 2) * 64 + row // 32 * 8 + row % 8
    wanted = jnp.sum(jnp.where(iota((256, 128), 1) == parcel, source, 0.0), axis=1, keepdims=True)
    wanted = wanted.astype(I32) + iota((256, 1), 0) // 8 % 4 * 4
    pick_ref[...] = jnp.where(iota((256, 512), 1) == wanted, 1.0, 0.0).astype(BF)
    dates = (iota((32, 256), 1) // 8 == iota((32, 256), 0)).astype(BF)
    clouds = mm(cloud_ref[...].astype(F32).astype(BF), dates)
    own_row = iota((8, 256), 0) == iota((8, 256), 1) % 8
    cloudy = jnp.sum(jnp.where(own_row, clouds, 0.0), axis=0, keepdims=True)
    qi = iota((256, 256), 0)
    ki = iota((256, 256), 1)
    mask_ref[...] = jnp.where((qi % 8 == ki % 8) & ((qi == ki) | (cloudy == 0.0)), 1.0, 0.0)
    head = iota((1, 1024), 1) // 64
    scale = jnp.zeros((1, 1024), F32)
    for i in range(16):
        scale = jnp.where(head == i, scale_ref[i] * LOG2E, scale)
    copies[2].wait()
    gain = gain_ref[...].astype(F32)
    gain = jnp.concatenate([gain[i : i + 1] for i in range(8)], axis=1)
    row_ref[...] = jnp.where(iota((8, 1024), 0) == 0, scale, gain)
    for copy in copies[3:]:
        copy.wait()


def prepare(block, scale, after, owner, cloud, gain, code, w_embed):
    return pl.pallas_call(
        prepare_kernel,
        out_shape=(
            jax.ShapeDtypeStruct((256, 512), BF),
            jax.ShapeDtypeStruct((256, 256), F32),
            jax.ShapeDtypeStruct((8, 1024), F32),
            jax.ShapeDtypeStruct((32, 1024), F32),
            jax.ShapeDtypeStruct((256, 1024), BF),
        ),
        in_specs=[pl.BlockSpec(memory_space=pltpu.SMEM)] * 2
        + [pl.BlockSpec(memory_space=pl.ANY)] * 6,
        out_specs=(pl.BlockSpec(memory_space=pltpu.VMEM),) * 5,
        scratch_shapes=[
            pltpu.VMEM((16, 128), I32),
            pltpu.VMEM((8, 32), I32),
            pltpu.VMEM((8, 128), BF),
            pltpu.SemaphoreType.DMA((5,)),
        ],
        compiler_params=pltpu.CompilerParams(vmem_limit_bytes=48 << 20),
        cost_estimate=pl.CostEstimate(flops=0, bytes_accessed=8 << 20, transcendentals=0),
        name="prepare",
    )(block, scale, after, owner, cloud, gain, code, w_embed)


def pick_kernel(pick_ref, rows_ref, out_ref):
    rows = rows_ref[...].reshape(512, 256)
    out_ref[...] = mm(pick_ref[...], rows).astype(BF).reshape(8, 32, 256)


def pick_rows(pick, rows):
    vmem = pl.BlockSpec(memory_space=pltpu.VMEM)
    return pl.pallas_call(
        pick_kernel,
        out_shape=jax.ShapeDtypeStruct((8, 32, 256), BF),
        in_specs=[vmem] * 2,
        out_specs=vmem,
        compiler_params=pltpu.CompilerParams(vmem_limit_bytes=16 << 20),
        name="pick_rows",
    )(pick, rows)


def attend_kernel(
    tok_ref, mask_ref, row_ref, code_ref, we_ref, wqkv_any, wo_any,
    emb_ref, all_ref, w_ref, wo_ref, sems,
):
    chunks = [
        [
            pltpu.make_async_copy(
                wqkv_any.at[:, 1024 * part + 256 * c : 1024 * part + 256 * c + 256],
                w_ref.at[c, :, 256 * part : 256 * part + 256],
                sems.at[3 * c + part],
            )
            for part in range(3)
        ]
        for c in range(4)
    ]
    chunks.append([pltpu.make_async_copy(wo_any, wo_ref, sems.at[12])])

    def start(number):
        for copy in chunks[number]:
            copy.start()

    start(0)
    encoded = mm(tok_ref[...], we_ref[...]).astype(BF).astype(F32)
    code = jnp.broadcast_to(code_ref[...][:, None, :], (32, 8, 1024)).reshape(256, 1024)
    state = encoded + code
    start(1)
    state_mean = jnp.mean(state.reshape(32, 8, 1024), axis=0)
    center = jnp.mean(state, axis=1, keepdims=True)
    moved = state - center
    spread = jnp.mean(moved * moved, axis=1, keepdims=True)
    normed = (moved * lax.rsqrt(spread + 1e-05) * row_ref[1:2, :]).astype(BF)

    seg = (iota((256, 256), 0) // 64 == iota((256, 256), 1) // 64).astype(BF)
    mask = mask_ref[...]
    left = iota((256, 128), 1) < 64
    ones = jnp.ones((256, 128), BF)
    none = jnp.zeros((256, 128), BF)
    means = []
    for c in range(4):
        for copy in chunks[c]:
            copy.wait()
        if c < 3:
            start(c + 2)
        queries = mm(normed, w_ref[c, :, 0:256])
        keys = mm(normed, w_ref[c, :, 256:512])
        values = mm(normed, w_ref[c, :, 512:768]).astype(BF)
        q_sum = mm((queries * queries).astype(BF), seg)
        k_sum = mm((keys * keys).astype(BF), seg)
        queries = (queries * (
            lax.rsqrt(q_sum + 1e-06) * row_ref[0:1, 256 * c : 256 * c + 256]
        )).astype(BF)
        keys = (keys * lax.rsqrt(k_sum + 1e-06)).astype(BF)
        for pair in range(2):
            lanes = slice(128 * pair, 128 * pair + 128)
            q_pair = queries[:, lanes]
            k_pair = keys[:, lanes]
            right = jnp.concatenate([values[:, lanes], ones], axis=1)
            mixed = []
            for side in range(2):
                k_side = jnp.where(left, k_pair, none) if side == 0 else jnp.where(left, none, k_pair)
                weights = (jnp.exp2(mm_nt(q_pair, k_side)) * mask).astype(BF)
                both = mm(weights, right)
                mixed.append(both[:, 0:128] / both[:, 128:256])
            means.append(jnp.mean(jnp.where(left, mixed[0], mixed[1]).reshape(32, 8, 128), axis=0))
    mean = jnp.concatenate(means, axis=1)
    high = mean.astype(BF)
    low = (mean - high.astype(F32)).astype(BF)
    chunks[4][0].wait()
    update = mm(jnp.concatenate([high, low], axis=0), wo_ref[...])
    embedding = (state_mean + (update[0:8] + update[8:16])).astype(BF)
    emb_ref[...] = embedding
    all_ref[...] = jnp.broadcast_to(embedding[None], (32, 8, 1024))


def attend(tokens, mask, rows, code, w_embed, w_qkv, w_out):
    vmem = pl.BlockSpec(memory_space=pltpu.VMEM)
    return pl.pallas_call(
        attend_kernel,
        out_shape=(
            jax.ShapeDtypeStruct((8, 1024), BF),
            jax.ShapeDtypeStruct((32, 8, 1024), BF),
        ),
        in_specs=[vmem] * 5 + [pl.BlockSpec(memory_space=pl.ANY)] * 2,
        out_specs=(vmem, vmem),
        scratch_shapes=[
            pltpu.VMEM((4, 1024, 768), BF),
            pltpu.VMEM((1024, 1024), BF),
            pltpu.SemaphoreType.DMA((13,)),
        ],
        compiler_params=pltpu.CompilerParams(vmem_limit_bytes=52 << 20),
        name="attend",
    )(tokens, mask, rows, code, w_embed, w_qkv, w_out)


def contrast_kernel(scale_ref, block_ref, all_ref, pos_ref, neg_ref, out_ref):
    others = all_ref[...].reshape(256, 1024).astype(F32)
    square = others * others
    high = square.astype(BF)
    low = (square - high.astype(F32)).astype(BF)
    ones = jnp.ones((8, 1024), BF)
    other_sum = mm_nt(ones, high) + mm_nt(ones, low)
    mine = all_ref[block_ref[0]]
    anchors = mine.astype(F32)
    own_sum = jnp.sum(anchors * anchors, axis=1, keepdims=True)
    similarity = mm_nt(mine, all_ref[...].reshape(256, 1024))
    similarity = similarity * lax.rsqrt(own_sum + 1e-06) * lax.rsqrt(other_sum + 1e-06)
    logits = similarity * scale_ref[0]
    member = iota((8, 256), 1)
    positive = jnp.sum(jnp.where(member == pos_ref[...], logits, 0.0), axis=1, keepdims=True)
    ids = neg_ref[...]
    within = ids % 128
    near = jnp.take_along_axis(logits[:, 0:128], within, axis=1)
    far = jnp.take_along_axis(logits[:, 128:256], within, axis=1)
    negative = jnp.where(ids < 128, near, far)
    loss = jnp.log(1.0 + jnp.sum(jnp.exp(negative - positive), axis=1, keepdims=True))
    diagonal = iota((8, 128), 0) == iota((8, 128), 1)
    out_ref[...] = jnp.sum(jnp.where(diagonal, loss, 0.0), axis=0, keepdims=True)[:, 0:8]


def contrast(scale, block, others, pos_ids, neg_ids):
    vmem = pl.BlockSpec(memory_space=pltpu.VMEM)
    return pl.pallas_call(
        contrast_kernel,
        out_shape=jax.ShapeDtypeStruct((1, 8), F32),
        in_specs=[pl.BlockSpec(memory_space=pltpu.SMEM)] * 2 + [vmem] * 3,
        out_specs=vmem,
        compiler_params=pltpu.CompilerParams(vmem_limit_bytes=16 << 20),
        name="contrast",
    )(scale, block, others, pos_ids, neg_ids)


def date_code(dates, width):
    steps = np.arange(dates, dtype=np.float64)[:, None]
    pair = np.arange(width // 2, dtype=np.float64)[None, :]
    angles = steps * np.exp(-2.0 * pair / width * np.log(10000.0))
    table = np.stack([np.sin(angles), np.cos(angles)], axis=-1).reshape(dates, width)
    return table.astype(np.float32)


def per_device(
    tile_pixels,
    owner,
    pix_count,
    cloud,
    w_pix1,
    w_pix2,
    w_embed,
    norm_gain,
    w_qkv,
    w_out,
    head_scale,
    logit_scale,
    pos_ids,
    neg_ids,
):
    block = lax.axis_index("parcel").reshape(1).astype(I32)
    owner = owner.reshape(16, 128)
    pooled = pool_slots(
        block, tile_pixels, owner, pix_count.reshape(16, 128), w_pix1, w_pix2
    )
    arrived = lax.all_to_all(pooled, "parcel", split_axis=0, concat_axis=0, tiled=True)
    code = jnp.asarray(date_code(32, 1024))
    pick, mask, rows, code, w_embed = prepare(
        block, head_scale, pooled, owner, cloud, norm_gain.reshape(8, 128), code, w_embed
    )
    moving = pick_rows(pick, arrived)
    tokens = lax.all_to_all(moving, "date", split_axis=0, concat_axis=0, tiled=True)
    embedding, copies = attend(
        tokens.reshape(256, 256),
        mask,
        rows,
        code,
        w_embed,
        w_qkv,
        w_out,
    )
    others = lax.all_to_all(copies, "parcel", split_axis=0, concat_axis=0, tiled=True)
    loss = contrast(logit_scale, block, others, pos_ids.reshape(8, 1), neg_ids)
    return (embedding, loss.reshape(8))


def solution(mesh):
    in_specs = (
        P("date", "parcel", None),
        P(),
        P(),
        P(("parcel", "date"), None),
        P(),
        P(),
        P(),
        P(),
        P(),
        P(),
        P(),
        P(),
        P(("parcel", "date")),
        P(("parcel", "date"), None),
    )
    out_specs = (P(("parcel", "date"), None), P(("parcel", "date")))
    return jax.shard_map(
        per_device, mesh=mesh, in_specs=in_specs, out_specs=out_specs, check_vma=False
    )
```

```python
import jax
import jax.numpy as jnp
import numpy as np
from jax import lax
from jax.experimental import pallas as pl
from jax.experimental.pallas import tpu as pltpu
from jax.sharding import PartitionSpec as P

PAR_DEV = 64
CAP = 4
SETS = 64
BF = jnp.bfloat16
F32 = jnp.float32
I32 = jnp.int32
LOG2E = 1.4426950408889634


def iota(shape, dim):
    return lax.broadcasted_iota(I32, shape, dim)


def mm(left, right):
    return jnp.dot(left, right, preferred_element_type=F32)


def mm_nt(left, right):
    return lax.dot_general(left, right, (((1,), (1,)), ((), ())), preferred_element_type=F32)


def rep(block, times):
    return jnp.concatenate([block] * times, axis=0)


def pool_kernel(
    tile_ref, x_any, own_any, cnt_any, w1_any, w2_any, out_ref, done_ref,
    x_ref, own_ref, cnt_ref, w1_ref, w2_ref, w1s, ps, sems,
):
    rows = 4 * 128
    pairs = [(w1_any, w1_ref), (own_any, own_ref), (cnt_any, cnt_ref), (w2_any, w2_ref), (x_any, x_ref)]
    copies = [pltpu.make_async_copy(a, b, sems.at[i]) for i, (a, b) in enumerate(pairs)]
    for copy in copies:
        copy.start()
    done_ref[0] = tile_ref[0]
    w1s[...] = jnp.zeros((32, 256, 256), BF)
    li = iota((128, 128), 0)
    lj = iota((128, 128), 1)
    before = ((li < lj) & ((li // 64) == (lj // 64))).astype(BF)
    to_all = ((iota((128, 640), 1) % 10) == iota((128, 640), 0)).astype(BF)
    channel = (iota((640, 16), 0) % 10 == iota((640, 16), 1)).astype(BF)
    po = iota((256, 256), 0)
    pi = iota((256, 256), 1)
    order = ((po // 16 == pi // 4 % 16) & (po // 4 % 4 == pi // 64) & (po % 4 == pi % 4)).astype(BF)

    copies[0].wait()
    w1 = jnp.concatenate([w1_ref[...].astype(F32), jnp.zeros((6, 128), F32)], axis=0)
    tiled = mm(channel, w1.astype(BF))
    windows = []
    for j in range(SETS // 2):
        low = 20 * j
        start = low // 128 * 128
        windows.append((start, 256 if low + 20 > start + 128 else 128))
        top = low // 16 * 16
        end = -(-(low + 20) // 16) * 16
        part = tiled[top:end]
        row = iota((end - top, 128), 0) + top
        w1s[j, top - start : end - start, 0:128] = jnp.where(
            (row >= low) & (row < low + 10), part, 0.0
        ).astype(BF)
        w1s[j, top - start : end - start, 128:256] = jnp.where(
            (row >= low + 10) & (row < low + 20), part, 0.0
        ).astype(BF)

    copies[1].wait()
    copies[2].wait()
    match = own_ref[...] == tile_ref[0]
    rank = mm(match.astype(F32).astype(BF), before)
    code = jnp.where(match, rank.astype(I32), -1)
    sub = iota((16, 8, 128), 1)
    lane = iota((16, 8, 128), 2)
    hit = (code[:, None, :] == (sub % 4)) & ((lane // 64) == (sub // 4))
    amount = jnp.where(hit, cnt_ref[...][:, None, :], 0).reshape(128, 128)
    counts = mm(amount.astype(F32).astype(BF), jnp.ones((128, 128), BF))

    copies[3].wait()
    zero = jnp.zeros((128, 128), BF)
    w2 = w2_ref[...]
    w2 = jnp.concatenate(
        [jnp.concatenate([w2, zero], axis=1), jnp.concatenate([zero, w2], axis=1)], axis=0
    )

    copies[4].wait()
    x = x_ref[...].reshape(rows, 640)
    valid = (iota((128, 640), 1) // 10).astype(F32) < jnp.concatenate([counts] * 5, axis=1)
    first = mm(x[:, 0:128], to_all)
    ps[...] = jnp.where(rep(valid, 4), x.astype(F32), first).astype(BF)
    origin = total = square = None
    for j, (start, depth) in enumerate(windows):
        hidden = mm(ps[:, start : start + depth], w1s[j, 0:depth, :])
        hidden = jnp.maximum(hidden.astype(BF), 0)
        hidden = jnp.maximum(mm(hidden, w2), 0.0)
        if j == 0:
            origin = hidden[:, 0:128]
            total = hidden[:, 128:256] - origin
            square = total * total
        else:
            even = hidden[:, 0:128] - origin
            odd = hidden[:, 128:256] - origin
            total = total + (even + odd)
            square = square + (even * even + odd * odd)
    number = jnp.maximum(rep(counts, 4), 1.0)
    shift = total / number
    deviation = jnp.sqrt(jnp.maximum(square / number - shift * shift, 0.01))
    pooled = jnp.concatenate([origin + shift, deviation], axis=1).astype(BF)
    for half in range(2):
        part = jnp.concatenate(
            [pooled[d * 128 + half * 64 : d * 128 + half * 64 + 64] for d in range(4)], axis=0
        )
        out_ref[half * 16 : half * 16 + 16] = mm(order, part).astype(BF).reshape(16, 16, 256)


def pool_slots(tile, pixels, owner, counts, w_pix1, w_pix2):
    return pl.pallas_call(
        pool_kernel,
        out_shape=(jax.ShapeDtypeStruct((32, 16, 256), BF), jax.ShapeDtypeStruct((1,), I32)),
        in_specs=[pl.BlockSpec(memory_space=pltpu.SMEM)] + [pl.BlockSpec(memory_space=pl.ANY)] * 5,
        out_specs=(pl.BlockSpec(memory_space=pltpu.VMEM), pl.BlockSpec(memory_space=pltpu.SMEM)),
        scratch_shapes=[
            pltpu.VMEM((4, 128, 640), BF),
            pltpu.VMEM((16, 128), I32),
            pltpu.VMEM((16, 128), I32),
            pltpu.VMEM((10, 128), BF),
            pltpu.VMEM((128, 128), BF),
            pltpu.VMEM((32, 256, 256), BF),
            pltpu.VMEM((512, 640), BF),
            pltpu.SemaphoreType.DMA((5,)),
        ],
        compiler_params=pltpu.CompilerParams(vmem_limit_bytes=60 << 20),
        name="pool_slots",
    )(tile, pixels, owner, counts, w_pix1, w_pix2)


def prepare_kernel(
    block_ref, scale_ref, own_any, cloud_any, gain_any, code_any, we_any,
    pick_ref, mask_ref, row_ref, code_ref, we_ref, own_ref, cloud_ref, gain_ref, sems,
):
    pairs = [
        (own_any, own_ref),
        (cloud_any, cloud_ref),
        (gain_any, gain_ref),
        (we_any, we_ref),
        (code_any, code_ref),
    ]
    copies = [pltpu.make_async_copy(a, b, sems.at[i]) for i, (a, b) in enumerate(pairs)]
    for copy in copies:
        copy.start()
    copies[0].wait()
    copies[1].wait()
    block = block_ref[0]
    owner = own_ref[pl.ds(block // 2, 1), :].astype(F32)
    sub = iota((128, 128), 0)
    lane = iota((128, 128), 1)
    column = jnp.sum(jnp.where(sub == lane, owner, 0.0), axis=1, keepdims=True)
    earlier = (column == owner) & (sub < lane) & (sub // 64 == lane // 64)
    rank = jnp.sum(jnp.where(earlier, 1.0, 0.0), axis=0, keepdims=True)
    source = owner * 16.0 + rank
    row = iota((256, 128), 0)
    parcel = (block % 2) * 64 + row // 32 * 8 + row % 8
    wanted = jnp.sum(jnp.where(iota((256, 128), 1) == parcel, source, 0.0), axis=1, keepdims=True)
    wanted = wanted.astype(I32) + iota((256, 1), 0) // 8 % 4 * 4
    pick_ref[...] = jnp.where(iota((256, 512), 1) == wanted, 1.0, 0.0).astype(BF)
    dates = (iota((32, 256), 1) // 8 == iota((32, 256), 0)).astype(BF)
    clouds = mm(cloud_ref[...].astype(F32).astype(BF), dates)
    own_row = iota((8, 256), 0) == iota((8, 256), 1) % 8
    cloudy = jnp.sum(jnp.where(own_row, clouds, 0.0), axis=0, keepdims=True)
    qi = iota((256, 256), 0)
    ki = iota((256, 256), 1)
    mask_ref[...] = jnp.where((qi % 8 == ki % 8) & ((qi == ki) | (cloudy == 0.0)), 1.0, 0.0)
    head = iota((1, 1024), 1) // 64
    scale = jnp.zeros((1, 1024), F32)
    for i in range(16):
        scale = jnp.where(head == i, scale_ref[i] * LOG2E, scale)
    copies[2].wait()
    gain = gain_ref[...].astype(F32)
    gain = jnp.concatenate([gain[i : i + 1] for i in range(8)], axis=1)
    row_ref[...] = jnp.where(iota((8, 1024), 0) == 0, scale, gain)
    for copy in copies[3:]:
        copy.wait()


def prepare(block, scale, owner, cloud, gain, code, w_embed):
    return pl.pallas_call(
        prepare_kernel,
        out_shape=(
            jax.ShapeDtypeStruct((256, 512), BF),
            jax.ShapeDtypeStruct((256, 256), F32),
            jax.ShapeDtypeStruct((8, 1024), F32),
            jax.ShapeDtypeStruct((32, 1024), F32),
            jax.ShapeDtypeStruct((256, 1024), BF),
        ),
        in_specs=[pl.BlockSpec(memory_space=pltpu.SMEM)] * 2
        + [pl.BlockSpec(memory_space=pl.ANY)] * 5,
        out_specs=(pl.BlockSpec(memory_space=pltpu.VMEM),) * 5,
        scratch_shapes=[
            pltpu.VMEM((16, 128), I32),
            pltpu.VMEM((8, 32), I32),
            pltpu.VMEM((8, 128), BF),
            pltpu.SemaphoreType.DMA((5,)),
        ],
        compiler_params=pltpu.CompilerParams(vmem_limit_bytes=48 << 20),
        cost_estimate=pl.CostEstimate(flops=0, bytes_accessed=8 << 20, transcendentals=0),
        name="prepare",
    )(block, scale, owner, cloud, gain, code, w_embed)


def pick_kernel(pick_ref, rows_ref, out_ref):
    rows = rows_ref[...].reshape(512, 256)
    out_ref[...] = mm(pick_ref[...], rows).astype(BF).reshape(8, 32, 256)


def pick_rows(pick, rows):
    vmem = pl.BlockSpec(memory_space=pltpu.VMEM)
    return pl.pallas_call(
        pick_kernel,
        out_shape=jax.ShapeDtypeStruct((8, 32, 256), BF),
        in_specs=[vmem] * 2,
        out_specs=vmem,
        compiler_params=pltpu.CompilerParams(vmem_limit_bytes=16 << 20),
        name="pick_rows",
    )(pick, rows)


def attend_kernel(
    tok_ref, mask_ref, row_ref, code_ref, we_ref, wqkv_any, wo_any,
    emb_ref, all_ref, w_ref, wo_ref, sems,
):
    chunks = [
        [
            pltpu.make_async_copy(
                wqkv_any.at[:, 1024 * part + 256 * c : 1024 * part + 256 * c + 256],
                w_ref.at[c, :, 256 * part : 256 * part + 256],
                sems.at[3 * c + part],
            )
            for part in range(3)
        ]
        for c in range(4)
    ]
    chunks.append([pltpu.make_async_copy(wo_any, wo_ref, sems.at[12])])

    def start(number):
        for copy in chunks[number]:
            copy.start()

    start(0)
    encoded = mm(tok_ref[...], we_ref[...]).astype(BF).astype(F32)
    code = jnp.broadcast_to(code_ref[...][:, None, :], (32, 8, 1024)).reshape(256, 1024)
    state = encoded + code
    start(1)
    state_mean = jnp.mean(state.reshape(32, 8, 1024), axis=0)
    center = jnp.mean(state, axis=1, keepdims=True)
    moved = state - center
    spread = jnp.mean(moved * moved, axis=1, keepdims=True)
    normed = (moved * lax.rsqrt(spread + 1e-05) * row_ref[1:2, :]).astype(BF)

    seg = (iota((256, 256), 0) // 64 == iota((256, 256), 1) // 64).astype(BF)
    mask = mask_ref[...]
    left = iota((256, 128), 1) < 64
    ones = jnp.ones((256, 128), BF)
    none = jnp.zeros((256, 128), BF)
    means = []

    def project(c):
        for copy in chunks[c]:
            copy.wait()
        if c < 3:
            start(c + 2)
        queries = mm(normed, w_ref[c, :, 0:256])
        keys = mm(normed, w_ref[c, :, 256:512])
        values = mm(normed, w_ref[c, :, 512:768]).astype(BF)
        q_sum = mm((queries * queries).astype(BF), seg)
        k_sum = mm((keys * keys).astype(BF), seg)
        scale = row_ref[0:1, 256 * c : 256 * c + 256]
        queries = (queries * (lax.rsqrt(q_sum + 1e-06) * scale)).astype(BF)
        keys = (keys * lax.rsqrt(k_sum + 1e-06)).astype(BF)
        return queries, keys, values

    def mix(queries, keys, values):
        for pair in range(2):
            lanes = slice(128 * pair, 128 * pair + 128)
            q_pair = queries[:, lanes]
            k_pair = keys[:, lanes]
            right = jnp.concatenate([values[:, lanes], ones], axis=1)
            mixed = []
            for side in range(2):
                k_side = jnp.where(left, k_pair, none) if side == 0 else jnp.where(left, none, k_pair)
                weights = (jnp.exp2(mm_nt(q_pair, k_side)) * mask).astype(BF)
                both = mm(weights, right)
                mixed.append(both[:, 0:128] / both[:, 128:256])
            means.append(jnp.mean(jnp.where(left, mixed[0], mixed[1]).reshape(32, 8, 128), axis=0))

    current = project(0)
    for c in range(1, 4):
        following = project(c)
        mix(*current)
        current = following
    mix(*current)
    mean = jnp.concatenate(means, axis=1)
    high = mean.astype(BF)
    low = (mean - high.astype(F32)).astype(BF)
    chunks[4][0].wait()
    update = mm(jnp.concatenate([high, low], axis=0), wo_ref[...])
    embedding = (state_mean + (update[0:8] + update[8:16])).astype(BF)
    emb_ref[...] = embedding
    all_ref[...] = jnp.broadcast_to(embedding[None], (32, 8, 1024))


def attend(tokens, mask, rows, code, w_embed, w_qkv, w_out):
    vmem = pl.BlockSpec(memory_space=pltpu.VMEM)
    return pl.pallas_call(
        attend_kernel,
        out_shape=(
            jax.ShapeDtypeStruct((8, 1024), BF),
            jax.ShapeDtypeStruct((32, 8, 1024), BF),
        ),
        in_specs=[vmem] * 5 + [pl.BlockSpec(memory_space=pl.ANY)] * 2,
        out_specs=(vmem, vmem),
        scratch_shapes=[
            pltpu.VMEM((4, 1024, 768), BF),
            pltpu.VMEM((1024, 1024), BF),
            pltpu.SemaphoreType.DMA((13,)),
        ],
        compiler_params=pltpu.CompilerParams(vmem_limit_bytes=52 << 20),
        name="attend",
    )(tokens, mask, rows, code, w_embed, w_qkv, w_out)


def contrast_kernel(scale_ref, block_ref, all_ref, pos_ref, neg_ref, out_ref, products):
    others = all_ref[...].reshape(256, 1024)
    products[...] = mm_nt(others, others)
    same = iota((256, 256), 0) == iota((256, 256), 1)
    other_sum = jnp.sum(jnp.where(same, products[...], 0.0), axis=0, keepdims=True)
    mine = pl.multiple_of(block_ref[0] * 8, 8)
    similarity = products[pl.ds(mine, 8), :]
    own = iota((8, 256), 1) == iota((8, 256), 0) + mine
    own_sum = jnp.sum(jnp.where(own, similarity, 0.0), axis=1, keepdims=True)
    similarity = similarity * lax.rsqrt(own_sum + 1e-06) * lax.rsqrt(other_sum + 1e-06)
    logits = similarity * scale_ref[0]
    member = iota((8, 256), 1)
    positive = jnp.sum(jnp.where(member == pos_ref[...], logits, 0.0), axis=1, keepdims=True)
    ids = neg_ref[...]
    within = ids % 128
    near = jnp.take_along_axis(logits[:, 0:128], within, axis=1)
    far = jnp.take_along_axis(logits[:, 128:256], within, axis=1)
    negative = jnp.where(ids < 128, near, far)
    loss = jnp.log(1.0 + jnp.sum(jnp.exp(negative - positive), axis=1, keepdims=True))
    diagonal = iota((8, 128), 0) == iota((8, 128), 1)
    out_ref[...] = jnp.sum(jnp.where(diagonal, loss, 0.0), axis=0, keepdims=True)[:, 0:8]


def contrast(scale, block, others, pos_ids, neg_ids):
    vmem = pl.BlockSpec(memory_space=pltpu.VMEM)
    return pl.pallas_call(
        contrast_kernel,
        out_shape=jax.ShapeDtypeStruct((1, 8), F32),
        in_specs=[pl.BlockSpec(memory_space=pltpu.SMEM)] * 2 + [vmem] * 3,
        out_specs=vmem,
        scratch_shapes=[pltpu.VMEM((256, 256), F32)],
        compiler_params=pltpu.CompilerParams(vmem_limit_bytes=16 << 20),
        name="contrast",
    )(scale, block, others, pos_ids, neg_ids)


def date_code(dates, width):
    steps = np.arange(dates, dtype=np.float64)[:, None]
    pair = np.arange(width // 2, dtype=np.float64)[None, :]
    angles = steps * np.exp(-2.0 * pair / width * np.log(10000.0))
    table = np.stack([np.sin(angles), np.cos(angles)], axis=-1).reshape(dates, width)
    return table.astype(np.float32)


def per_device(
    tile_pixels,
    owner,
    pix_count,
    cloud,
    w_pix1,
    w_pix2,
    w_embed,
    norm_gain,
    w_qkv,
    w_out,
    head_scale,
    logit_scale,
    pos_ids,
    neg_ids,
):
    block = lax.axis_index("parcel").reshape(1).astype(I32)
    owner = owner.reshape(16, 128)
    pooled, place = pool_slots(
        block, tile_pixels, owner, pix_count.reshape(16, 128), w_pix1, w_pix2
    )
    arrived = lax.all_to_all(pooled, "parcel", split_axis=0, concat_axis=0, tiled=True)
    code = jnp.asarray(date_code(32, 1024))
    pick, mask, rows, code, w_embed = prepare(
        place, head_scale, owner, cloud, norm_gain.reshape(8, 128), code, w_embed
    )
    moving = pick_rows(pick, arrived)
    tokens = lax.all_to_all(moving, "date", split_axis=0, concat_axis=0, tiled=True)
    embedding, copies = attend(
        tokens.reshape(256, 256),
        mask,
        rows,
        code,
        w_embed,
        w_qkv,
        w_out,
    )
    others = lax.all_to_all(copies, "parcel", split_axis=0, concat_axis=0, tiled=True)
    loss = contrast(logit_scale, block, others, pos_ids.reshape(8, 1), neg_ids)
    return (embedding, loss.reshape(8))


def solution(mesh):
    in_specs = (
        P("date", "parcel", None),
        P(),
        P(),
        P(("parcel", "date"), None),
        P(),
        P(),
        P(),
        P(),
        P(),
        P(),
        P(),
        P(),
        P(("parcel", "date")),
        P(("parcel", "date"), None),
    )
    out_specs = (P(("parcel", "date"), None), P(("parcel", "date")))
    return jax.shard_map(
        per_device, mesh=mesh, in_specs=in_specs, out_specs=out_specs, check_vma=False
    )
```

```python
import jax
import jax.numpy as jnp
import numpy as np
from jax import lax
from jax.experimental import pallas as pl
from jax.experimental.pallas import tpu as pltpu
from jax.sharding import PartitionSpec as P

PAR_DEV = 64
CAP = 4
SETS = 64
BF = jnp.bfloat16
F32 = jnp.float32
I32 = jnp.int32
LOG2E = 1.4426950408889634


def iota(shape, dim):
    return lax.broadcasted_iota(I32, shape, dim)


def mm(left, right):
    return jnp.dot(left, right, preferred_element_type=F32)


def mm_nt(left, right):
    return lax.dot_general(left, right, (((1,), (1,)), ((), ())), preferred_element_type=F32)


def rep(block, times):
    return jnp.concatenate([block] * times, axis=0)


def pool_kernel(
    tile_ref, x_any, own_any, cnt_any, w1_any, w2_any, out_ref, done_ref,
    x_ref, own_ref, cnt_ref, w1_ref, w2_ref, w1s, ps, sems,
):
    rows = 4 * 128
    pairs = [(w1_any, w1_ref), (own_any, own_ref), (cnt_any, cnt_ref), (w2_any, w2_ref), (x_any, x_ref)]
    copies = [pltpu.make_async_copy(a, b, sems.at[i]) for i, (a, b) in enumerate(pairs)]
    for copy in copies:
        copy.start()
    done_ref[0] = tile_ref[0]
    w1s[...] = jnp.zeros((32, 256, 256), BF)
    li = iota((128, 128), 0)
    lj = iota((128, 128), 1)
    before = ((li < lj) & ((li // 64) == (lj // 64))).astype(BF)
    to_all = ((iota((128, 640), 1) % 10) == iota((128, 640), 0)).astype(BF)
    channel = (iota((640, 16), 0) % 10 == iota((640, 16), 1)).astype(BF)
    po = iota((256, 256), 0)
    pi = iota((256, 256), 1)
    order = ((po // 16 == pi // 4 % 16) & (po // 4 % 4 == pi // 64) & (po % 4 == pi % 4)).astype(BF)

    copies[0].wait()
    w1 = jnp.concatenate([w1_ref[...].astype(F32), jnp.zeros((6, 128), F32)], axis=0)
    tiled = mm(channel, w1.astype(BF))
    windows = []
    for j in range(SETS // 2):
        low = 20 * j
        start = low // 128 * 128
        windows.append((start, 256 if low + 20 > start + 128 else 128))
        top = low // 16 * 16
        end = -(-(low + 20) // 16) * 16
        part = tiled[top:end]
        row = iota((end - top, 128), 0) + top
        w1s[j, top - start : end - start, 0:128] = jnp.where(
            (row >= low) & (row < low + 10), part, 0.0
        ).astype(BF)
        w1s[j, top - start : end - start, 128:256] = jnp.where(
            (row >= low + 10) & (row < low + 20), part, 0.0
        ).astype(BF)

    copies[1].wait()
    copies[2].wait()
    match = own_ref[...] == tile_ref[0]
    rank = mm(match.astype(F32).astype(BF), before)
    code = jnp.where(match, rank.astype(I32), -1)
    sub = iota((16, 8, 128), 1)
    lane = iota((16, 8, 128), 2)
    hit = (code[:, None, :] == (sub % 4)) & ((lane // 64) == (sub // 4))
    amount = jnp.where(hit, cnt_ref[...][:, None, :], 0).reshape(128, 128)
    counts = mm(amount.astype(F32).astype(BF), jnp.ones((128, 128), BF))

    copies[3].wait()
    zero = jnp.zeros((128, 128), BF)
    w2 = w2_ref[...]
    w2 = jnp.concatenate(
        [jnp.concatenate([w2, zero], axis=1), jnp.concatenate([zero, w2], axis=1)], axis=0
    )

    copies[4].wait()
    x = x_ref[...].reshape(rows, 640)
    valid = (iota((128, 640), 1) // 10).astype(F32) < jnp.concatenate([counts] * 5, axis=1)
    first = mm(x[:, 0:128], to_all)
    ps[...] = jnp.where(rep(valid, 4), x.astype(F32), first).astype(BF)
    origin = total = square = None
    for j, (start, depth) in enumerate(windows):
        hidden = mm(ps[:, start : start + depth], w1s[j, 0:depth, :])
        hidden = jnp.maximum(hidden.astype(BF), 0)
        hidden = jnp.maximum(mm(hidden, w2), 0.0)
        if j == 0:
            origin = hidden[:, 0:128]
            total = hidden[:, 128:256] - origin
            square = total * total
        else:
            even = hidden[:, 0:128] - origin
            odd = hidden[:, 128:256] - origin
            total = total + (even + odd)
            square = square + (even * even + odd * odd)
    number = jnp.maximum(rep(counts, 4), 1.0)
    shift = total / number
    deviation = jnp.sqrt(jnp.maximum(square / number - shift * shift, 0.01))
    pooled = jnp.concatenate([origin + shift, deviation], axis=1).astype(BF)
    for half in range(2):
        part = jnp.concatenate(
            [pooled[d * 128 + half * 64 : d * 128 + half * 64 + 64] for d in range(4)], axis=0
        )
        out_ref[half * 16 : half * 16 + 16] = mm(order, part).astype(BF).reshape(16, 16, 256)


def pool_slots(tile, pixels, owner, counts, w_pix1, w_pix2):
    return pl.pallas_call(
        pool_kernel,
        out_shape=(jax.ShapeDtypeStruct((32, 16, 256), BF), jax.ShapeDtypeStruct((1,), I32)),
        in_specs=[pl.BlockSpec(memory_space=pltpu.SMEM)] + [pl.BlockSpec(memory_space=pl.ANY)] * 5,
        out_specs=(pl.BlockSpec(memory_space=pltpu.VMEM), pl.BlockSpec(memory_space=pltpu.SMEM)),
        scratch_shapes=[
            pltpu.VMEM((4, 128, 640), BF),
            pltpu.VMEM((16, 128), I32),
            pltpu.VMEM((16, 128), I32),
            pltpu.VMEM((10, 128), BF),
            pltpu.VMEM((128, 128), BF),
            pltpu.VMEM((32, 256, 256), BF),
            pltpu.VMEM((512, 640), BF),
            pltpu.SemaphoreType.DMA((5,)),
        ],
        compiler_params=pltpu.CompilerParams(vmem_limit_bytes=60 << 20),
        name="pool_slots",
    )(tile, pixels, owner, counts, w_pix1, w_pix2)


def prepare_kernel(
    block_ref, scale_ref, own_any, cloud_any, gain_any, code_any, we_any,
    pick_ref, mask_ref, row_ref, code_ref, we_ref, own_ref, cloud_ref, gain_ref, sems,
):
    pairs = [
        (own_any, own_ref),
        (cloud_any, cloud_ref),
        (gain_any, gain_ref),
        (we_any, we_ref),
        (code_any, code_ref),
    ]
    copies = [pltpu.make_async_copy(a, b, sems.at[i]) for i, (a, b) in enumerate(pairs)]
    for copy in copies:
        copy.start()
    copies[0].wait()
    copies[1].wait()
    block = block_ref[0]
    owner = own_ref[pl.ds(block // 2, 1), :].astype(F32)
    sub = iota((128, 128), 0)
    lane = iota((128, 128), 1)
    column = jnp.sum(jnp.where(sub == lane, owner, 0.0), axis=1, keepdims=True)
    earlier = (column == owner) & (sub < lane) & (sub // 64 == lane // 64)
    rank = jnp.sum(jnp.where(earlier, 1.0, 0.0), axis=0, keepdims=True)
    source = owner * 16.0 + rank
    row = iota((256, 128), 0)
    parcel = (block % 2) * 64 + row // 32 * 8 + row % 8
    wanted = jnp.sum(jnp.where(iota((256, 128), 1) == parcel, source, 0.0), axis=1, keepdims=True)
    wanted = wanted.astype(I32) + iota((256, 1), 0) // 8 % 4 * 4
    pick_ref[...] = jnp.where(iota((256, 512), 1) == wanted, 1.0, 0.0).astype(BF)
    dates = (iota((32, 256), 1) // 8 == iota((32, 256), 0)).astype(BF)
    clouds = mm(cloud_ref[...].astype(F32).astype(BF), dates)
    own_row = iota((8, 256), 0) == iota((8, 256), 1) % 8
    cloudy = jnp.sum(jnp.where(own_row, clouds, 0.0), axis=0, keepdims=True)
    qi = iota((256, 256), 0)
    ki = iota((256, 256), 1)
    mask_ref[...] = jnp.where((qi % 8 == ki % 8) & ((qi == ki) | (cloudy == 0.0)), 1.0, 0.0)
    head = iota((1, 1024), 1) // 64
    scale = jnp.zeros((1, 1024), F32)
    for i in range(16):
        scale = jnp.where(head == i, scale_ref[i] * LOG2E, scale)
    copies[2].wait()
    gain = gain_ref[...].astype(F32)
    gain = jnp.concatenate([gain[i : i + 1] for i in range(8)], axis=1)
    row_ref[...] = jnp.where(iota((8, 1024), 0) == 0, scale, gain)
    for copy in copies[3:]:
        copy.wait()


def prepare(block, scale, owner, cloud, gain, code, w_embed):
    return pl.pallas_call(
        prepare_kernel,
        out_shape=(
            jax.ShapeDtypeStruct((256, 512), BF),
            jax.ShapeDtypeStruct((256, 256), F32),
            jax.ShapeDtypeStruct((8, 1024), F32),
            jax.ShapeDtypeStruct((32, 1024), F32),
            jax.ShapeDtypeStruct((256, 1024), BF),
        ),
        in_specs=[pl.BlockSpec(memory_space=pltpu.SMEM)] * 2
        + [pl.BlockSpec(memory_space=pl.ANY)] * 5,
        out_specs=(pl.BlockSpec(memory_space=pltpu.VMEM),) * 5,
        scratch_shapes=[
            pltpu.VMEM((16, 128), I32),
            pltpu.VMEM((8, 32), I32),
            pltpu.VMEM((8, 128), BF),
            pltpu.SemaphoreType.DMA((5,)),
        ],
        compiler_params=pltpu.CompilerParams(vmem_limit_bytes=48 << 20),
        cost_estimate=pl.CostEstimate(flops=0, bytes_accessed=8 << 20, transcendentals=0),
        name="prepare",
    )(block, scale, owner, cloud, gain, code, w_embed)


def pick_kernel(pick_ref, rows_ref, out_ref):
    rows = rows_ref[...].reshape(512, 256)
    out_ref[...] = mm(pick_ref[...], rows).astype(BF).reshape(8, 32, 256)


def pick_rows(pick, rows):
    vmem = pl.BlockSpec(memory_space=pltpu.VMEM)
    return pl.pallas_call(
        pick_kernel,
        out_shape=jax.ShapeDtypeStruct((8, 32, 256), BF),
        in_specs=[vmem] * 2,
        out_specs=vmem,
        compiler_params=pltpu.CompilerParams(vmem_limit_bytes=16 << 20),
        name="pick_rows",
    )(pick, rows)


def attend_kernel(
    tok_ref, mask_ref, row_ref, code_ref, we_ref, wqkv_any, wo_any,
    emb_ref, all_ref, w_ref, wo_ref, sems,
):
    for c in range(4):
        for part in range(3):
            columns = pl.ds(1024 * part + 256 * c, 256)
            pltpu.make_async_copy(
                wqkv_any.at[:, columns],
                w_ref.at[c, :, 256 * part : 256 * part + 256],
                sems.at[c],
            ).start()
    last = pltpu.make_async_copy(wo_any, wo_ref, sems.at[4])
    last.start()
    encoded = mm(tok_ref[...], we_ref[...]).astype(BF).astype(F32)
    code = jnp.broadcast_to(code_ref[...][:, None, :], (32, 8, 1024)).reshape(256, 1024)
    state = encoded + code
    state_mean = jnp.mean(state.reshape(32, 8, 1024), axis=0)
    center = jnp.mean(state, axis=1, keepdims=True)
    moved = state - center
    spread = jnp.mean(moved * moved, axis=1, keepdims=True)
    normed = (moved * lax.rsqrt(spread + 1e-05) * row_ref[1:2, :]).astype(BF)

    seg = (iota((256, 256), 0) // 64 == iota((256, 256), 1) // 64).astype(BF)
    mask = mask_ref[...]
    left = iota((256, 128), 1) < 64
    ones = jnp.ones((256, 128), BF)
    none = jnp.zeros((256, 128), BF)
    means = []

    def project(c):
        for part in ((0,), (1,), (2, 3), ())[c]:
            pltpu.make_async_copy(w_ref.at[part], w_ref.at[part], sems.at[part]).wait()
        queries = mm(normed, w_ref[c, :, 0:256])
        keys = mm(normed, w_ref[c, :, 256:512])
        values = mm(normed, w_ref[c, :, 512:768]).astype(BF)
        q_sum = mm((queries * queries).astype(BF), seg)
        k_sum = mm((keys * keys).astype(BF), seg)
        scale = row_ref[0:1, 256 * c : 256 * c + 256]
        queries = (queries * (lax.rsqrt(q_sum + 1e-06) * scale)).astype(BF)
        keys = (keys * lax.rsqrt(k_sum + 1e-06)).astype(BF)
        return queries, keys, values

    def mix(queries, keys, values):
        for pair in range(2):
            lanes = slice(128 * pair, 128 * pair + 128)
            q_pair = queries[:, lanes]
            k_pair = keys[:, lanes]
            right = jnp.concatenate([values[:, lanes], ones], axis=1)
            mixed = []
            for side in range(2):
                k_side = jnp.where(left, k_pair, none) if side == 0 else jnp.where(left, none, k_pair)
                weights = (jnp.exp2(mm_nt(q_pair, k_side)) * mask).astype(BF)
                both = mm(weights, right)
                mixed.append(both[:, 0:128] / both[:, 128:256])
            means.append(jnp.mean(jnp.where(left, mixed[0], mixed[1]).reshape(32, 8, 128), axis=0))

    current = project(0)
    for c in range(1, 4):
        following = project(c)
        mix(*current)
        current = following
    mix(*current)
    mean = jnp.concatenate(means, axis=1)
    high = mean.astype(BF)
    low = (mean - high.astype(F32)).astype(BF)
    last.wait()
    update = mm(jnp.concatenate([high, low], axis=0), wo_ref[...])
    embedding = (state_mean + (update[0:8] + update[8:16])).astype(BF)
    emb_ref[...] = embedding
    all_ref[...] = jnp.broadcast_to(embedding[None], (32, 8, 1024))


def attend(tokens, mask, rows, code, w_embed, w_qkv, w_out):
    vmem = pl.BlockSpec(memory_space=pltpu.VMEM)
    return pl.pallas_call(
        attend_kernel,
        out_shape=(
            jax.ShapeDtypeStruct((8, 1024), BF),
            jax.ShapeDtypeStruct((32, 8, 1024), BF),
        ),
        in_specs=[vmem] * 5 + [pl.BlockSpec(memory_space=pl.ANY)] * 2,
        out_specs=(vmem, vmem),
        scratch_shapes=[
            pltpu.VMEM((4, 1024, 768), BF),
            pltpu.VMEM((1024, 1024), BF),
            pltpu.SemaphoreType.DMA((5,)),
        ],
        compiler_params=pltpu.CompilerParams(vmem_limit_bytes=52 << 20),
        name="attend",
    )(tokens, mask, rows, code, w_embed, w_qkv, w_out)


def contrast_kernel(scale_ref, block_ref, all_ref, pos_ref, neg_ref, out_ref, products):
    others = all_ref[...].reshape(256, 1024)
    products[...] = mm_nt(others, others)
    same = iota((256, 256), 0) == iota((256, 256), 1)
    other_sum = jnp.sum(jnp.where(same, products[...], 0.0), axis=0, keepdims=True)
    mine = pl.multiple_of(block_ref[0] * 8, 8)
    similarity = products[pl.ds(mine, 8), :]
    own = iota((8, 256), 1) == iota((8, 256), 0) + mine
    own_sum = jnp.sum(jnp.where(own, similarity, 0.0), axis=1, keepdims=True)
    similarity = similarity * lax.rsqrt(own_sum + 1e-06) * lax.rsqrt(other_sum + 1e-06)
    logits = similarity * scale_ref[0]
    member = iota((8, 256), 1)
    positive = jnp.sum(jnp.where(member == pos_ref[...], logits, 0.0), axis=1, keepdims=True)
    ids = neg_ref[...]
    within = ids % 128
    near = jnp.take_along_axis(logits[:, 0:128], within, axis=1)
    far = jnp.take_along_axis(logits[:, 128:256], within, axis=1)
    negative = jnp.where(ids < 128, near, far)
    loss = jnp.log(1.0 + jnp.sum(jnp.exp(negative - positive), axis=1, keepdims=True))
    diagonal = iota((8, 128), 0) == iota((8, 128), 1)
    out_ref[...] = jnp.sum(jnp.where(diagonal, loss, 0.0), axis=0, keepdims=True)[:, 0:8]


def contrast(scale, block, others, pos_ids, neg_ids):
    vmem = pl.BlockSpec(memory_space=pltpu.VMEM)
    return pl.pallas_call(
        contrast_kernel,
        out_shape=jax.ShapeDtypeStruct((1, 8), F32),
        in_specs=[pl.BlockSpec(memory_space=pltpu.SMEM)] * 2 + [vmem] * 3,
        out_specs=vmem,
        scratch_shapes=[pltpu.VMEM((256, 256), F32)],
        compiler_params=pltpu.CompilerParams(vmem_limit_bytes=16 << 20),
        name="contrast",
    )(scale, block, others, pos_ids, neg_ids)


def date_code(dates, width):
    steps = np.arange(dates, dtype=np.float64)[:, None]
    pair = np.arange(width // 2, dtype=np.float64)[None, :]
    angles = steps * np.exp(-2.0 * pair / width * np.log(10000.0))
    table = np.stack([np.sin(angles), np.cos(angles)], axis=-1).reshape(dates, width)
    return table.astype(np.float32)


def per_device(
    tile_pixels,
    owner,
    pix_count,
    cloud,
    w_pix1,
    w_pix2,
    w_embed,
    norm_gain,
    w_qkv,
    w_out,
    head_scale,
    logit_scale,
    pos_ids,
    neg_ids,
):
    block = lax.axis_index("parcel").reshape(1).astype(I32)
    owner = owner.reshape(16, 128)
    pooled, place = pool_slots(
        block, tile_pixels, owner, pix_count.reshape(16, 128), w_pix1, w_pix2
    )
    arrived = lax.all_to_all(pooled, "parcel", split_axis=0, concat_axis=0, tiled=True)
    code = jnp.asarray(date_code(32, 1024))
    pick, mask, rows, code, w_embed = prepare(
        place, head_scale, owner, cloud, norm_gain.reshape(8, 128), code, w_embed
    )
    moving = pick_rows(pick, arrived)
    tokens = lax.all_to_all(moving, "date", split_axis=0, concat_axis=0, tiled=True)
    embedding, copies = attend(
        tokens.reshape(256, 256),
        mask,
        rows,
        code,
        w_embed,
        w_qkv,
        w_out,
    )
    others = lax.all_to_all(copies, "parcel", split_axis=0, concat_axis=0, tiled=True)
    loss = contrast(logit_scale, block, others, pos_ids.reshape(8, 1), neg_ids)
    return (embedding, loss.reshape(8))


def solution(mesh):
    in_specs = (
        P("date", "parcel", None),
        P(),
        P(),
        P(("parcel", "date"), None),
        P(),
        P(),
        P(),
        P(),
        P(),
        P(),
        P(),
        P(),
        P(("parcel", "date")),
        P(("parcel", "date"), None),
    )
    out_specs = (P(("parcel", "date"), None), P(("parcel", "date")))
    return jax.shard_map(
        per_device, mesh=mesh, in_specs=in_specs, out_specs=out_specs, check_vma=False
    )
```
